256 devices in a mesh: lat: 8 (over x, y_hi), lon: 32 (over y_lo, z, core).
Axes of the slice: x: 4, y: 4 (y_hi: 2, y_lo: 2; y = y_hi * 2 + y_lo), z: 8, core: 2. Of those that a mesh axis runs over, the one named last changes fastest.
Arguments:
- latent: bfloat16 [48, 1536, 512], P('lat', 'lon'), may hold values from -6 to 6
- norm_gain: float32 [512], replicated, may hold values from 0.1 to 1.9
- w_qkv: bfloat16 [512, 1536], replicated, may hold values from -0.5 to 0.5
- w_out: bfloat16 [512, 512], replicated, may hold values from -0.25 to 0.25
- cotangent: bfloat16 [48, 1536, 512], P('lat', 'lon'), may hold values from -6 to 6
Outputs:
- mixed: bfloat16 [48, 1536, 512], P('lat', 'lon')
- d_latent: bfloat16 [48, 1536, 512], P('lat', 'lon')
- grad_qkv: float32 [512, 1536], replicated
- grad_out: float32 [512, 512], replicated
- grad_gain: float32 [512], replicated
The draws below stay inside these ranges and needn't reach their ends.
All inputs are finite; a program needn't handle non-finite values.
Results may differ from the reference program's by a relative error of at most 0.013.
Values may be sent and summed in bfloat16 or wider, within the bound.
No kernel may reach another device: no remote copies, remote signals or barrier semaphores. Data moves between devices by JAX's collectives and lax.ppermute only.
A program may use at most 64 MiB of HBM per device.

```python
import jax
import jax.numpy as jnp
from jax import lax

D = 512
HEADS = 16
HS = 32
WL = 6
WW = 12
NLAT = 48
NLON = 1536


def draw_w_qkv(key, part):
    key = jax.random.fold_in(key, 11)
    drawn = jax.random.normal(key, (D, 3 * D), jnp.float32) * D ** (-0.5)
    return jnp.clip(drawn, -0.5, 0.5).astype(jnp.bfloat16)


def levels(own_key, extent, pieces, low, top_value):
    level, own = 1.0, jax.random.fold_in(own_key, 6)
    for axis_at, shards_of in pieces:
        steps = jnp.exp(jax.random.uniform(jax.random.fold_in(own, axis_at), (shards_of,), jnp.float32, low / len(pieces), top_value / len(pieces)))
        level = level * jnp.repeat(steps, extent[axis_at] // shards_of).reshape([-1 if axis == axis_at else 1 for axis in range(len(extent))])
    return level


def normal_values(stream_key, dims, scale, most, split=(), dtype=jnp.bfloat16):
    drawn = scale * jax.random.normal(stream_key, dims, jnp.float32)
    if split:
        drawn = drawn * levels(stream_key, dims, split, -0.22, 0.18)
    return jnp.clip(drawn, -most, most).astype(dtype)


def setup_inputs(seed: int = 0) -> dict:
    seeds = jax.random.split(jax.random.key(seed), 6)
    latent = normal_values(seeds[0], (NLAT, NLON, D), 1.0, 6.0, ((0, 8), (1, 32)))
    norm_gain = jnp.clip(1.0 + 0.18 * jax.random.normal(seeds[1], (D,), jnp.float32), 0.1, 1.9)
    w_qkv = draw_w_qkv(jax.random.fold_in(seeds[5], 71), 0)
    w_out = normal_values(seeds[3], (D, D), D ** -0.5, 0.25)
    cotangent = normal_values(seeds[4], (NLAT, NLON, D), 1.0, 6.0, ((0, 8), (1, 32)))
    return dict(latent=latent, norm_gain=norm_gain, w_qkv=w_qkv, w_out=w_out, cotangent=cotangent)


def to_windows(field):
    height, breadth, features = field.shape
    blocks = field.reshape(height // WL, WL, breadth // WW, WW, features)
    return blocks.transpose(0, 2, 1, 3, 4).reshape(-1, WL * WW, features)

def from_windows(stacked, height, breadth):
    features = stacked.shape[-1]
    blocks = stacked.reshape(height // WL, breadth // WW, WL, WW, features)
    return blocks.transpose(0, 2, 1, 3, 4).reshape(height, breadth, features)

def attend(packed, d_context, region):
    win_count, win_size, _ = packed.shape
    parts = packed.astype(jnp.float32).reshape(win_count, win_size, 3, HEADS, HS)
    queries = parts[:, :, 0]
    key_rows = parts[:, :, 1]
    values = parts[:, :, 2]
    scaling = HS ** (-0.5)
    scores = jnp.einsum('bqhd,bkhd->bhqk', queries, key_rows) * scaling
    allowed = (region[:, :, None] == region[:, None, :])[:, None]
    masked = jnp.where(allowed, scores, -1e+30)
    row_max = lax.optimization_barrier(jnp.max(masked, axis=-1, keepdims=True))
    expo_terms = jnp.exp(masked - row_max)
    probs = expo_terms / lax.optimization_barrier(jnp.sum(expo_terms, axis=-1, keepdims=True))
    weights = probs.astype(jnp.bfloat16)
    weights_up = weights.astype(jnp.float32)
    context = jnp.einsum('bhqk,bkhd->bqhd', weights_up, values).astype(jnp.bfloat16)
    context = context.reshape(win_count, win_size, HEADS * HS)
    grad_ctx = d_context.astype(jnp.float32).reshape(win_count, win_size, HEADS, HS)
    d_weights = jnp.einsum('bqhd,bkhd->bhqk', grad_ctx, values)
    d_values = jnp.einsum('bhqk,bqhd->bkhd', weights_up, grad_ctx).astype(jnp.bfloat16)
    d_scores = probs * (d_weights - lax.optimization_barrier(jnp.sum(d_weights * probs, axis=-1, keepdims=True)))
    d_scaled = (d_scores * scaling).astype(jnp.bfloat16).astype(jnp.float32)
    d_queries = jnp.einsum('bhqk,bkhd->bqhd', d_scaled, key_rows).astype(jnp.bfloat16)
    d_key_rows = jnp.einsum('bhqk,bqhd->bkhd', d_scaled, queries).astype(jnp.bfloat16)
    d_packed = jnp.stack([d_queries, d_key_rows, d_values], axis=2)
    return (context, d_packed.reshape(win_count, win_size, 3 * HEADS * HS))

def reference(latent, norm_gain, w_qkv, w_out, cotangent):
    half_rows = WL // 2
    half_cols = WW // 2
    latent_f = latent.astype(jnp.float32)
    centred = latent_f - lax.optimization_barrier(jnp.mean(latent_f, axis=-1, keepdims=True))
    variance = lax.optimization_barrier(jnp.mean(centred * centred, axis=-1, keepdims=True))
    recip_std = lax.rsqrt(variance + 1e-05)
    normed = centred * recip_std
    scaled_in = (normed * norm_gain).astype(jnp.bfloat16)
    shifted_in = jnp.roll(scaled_in, (-half_rows, -half_cols), (0, 1))
    shifted_cot = jnp.roll(cotangent, (-half_rows, -half_cols), (0, 1))
    band_count = NLAT // WL
    band_in = shifted_in.reshape(band_count, WL, NLON, D)
    band_cot = shifted_cot.reshape(band_count, WL, NLON, D)
    region_rows = (jnp.arange(NLAT) >= NLAT - half_rows).astype(jnp.int32).reshape(band_count, WL)
    row_tokens = WL * NLON

    def band_step(carried, items):
        grad_qkv, grad_out = carried
        piece_in, piece_cot, piece_region = items
        flat_in = piece_in.reshape(row_tokens, D)
        flat_cot = piece_cot.reshape(row_tokens, D)
        packed = jnp.dot(flat_in, w_qkv, preferred_element_type=jnp.float32).astype(jnp.bfloat16)
        d_context = jnp.dot(flat_cot, w_out.T, preferred_element_type=jnp.float32).astype(jnp.bfloat16)
        region_grid = jnp.broadcast_to(piece_region[:, None, None], (WL, NLON, 1))
        region_win = to_windows(region_grid)[:, :, 0]
        context_w, d_packed_w = attend(to_windows(packed.reshape(WL, NLON, 3 * D)), to_windows(d_context.reshape(WL, NLON, D)), region_win)
        context_flat = from_windows(context_w, WL, NLON).reshape(row_tokens, D)
        attn_out = jnp.dot(context_flat, w_out, preferred_element_type=jnp.float32).astype(jnp.bfloat16)
        grad_out = grad_out + jnp.dot(context_flat.T, flat_cot, preferred_element_type=jnp.float32)
        d_packed_flat = from_windows(d_packed_w, WL, NLON).reshape(row_tokens, 3 * D)
        grad_qkv = grad_qkv + jnp.dot(flat_in.T, d_packed_flat, preferred_element_type=jnp.float32)
        d_shifted = jnp.dot(d_packed_flat, w_qkv.T, preferred_element_type=jnp.float32).astype(jnp.bfloat16)
        return ((grad_qkv, grad_out), (attn_out.reshape(WL, NLON, D), d_shifted.reshape(WL, NLON, D)))
    start = (jnp.zeros((D, 3 * D), jnp.float32), jnp.zeros((D, D), jnp.float32))
    (grad_qkv, grad_out), (attn_bands, d_bands) = lax.scan(band_step, start, (band_in, band_cot, region_rows))
    attn_moved = jnp.roll(attn_bands.reshape(NLAT, NLON, D), (half_rows, half_cols), (0, 1))
    d_moved = jnp.roll(d_bands.reshape(NLAT, NLON, D), (half_rows, half_cols), (0, 1)).astype(jnp.float32)
    mixed = (latent_f + attn_moved.astype(jnp.float32)).astype(jnp.bfloat16)
    grad_gain = lax.optimization_barrier(jnp.sum(d_moved * normed, axis=(0, 1)))
    hidden_grad = d_moved * norm_gain
    d_norm_part = recip_std * (hidden_grad - lax.optimization_barrier(jnp.mean(hidden_grad, axis=-1, keepdims=True)) - normed * lax.optimization_barrier(jnp.mean(hidden_grad * normed, axis=-1, keepdims=True)))
    d_latent = (cotangent.astype(jnp.float32) + d_norm_part).astype(jnp.bfloat16)
    return (mixed, d_latent, grad_qkv, grad_out, grad_gain)
```

```python
import jax
import jax.numpy as jnp
from jax import lax
from jax.sharding import Mesh, PartitionSpec as P

ALL = ("x", "yh", "yl", "z", "c")
LAT = ("x", "yh")
LON = ("yl", "z", "c")
HEADS = 16
HS = 32
WL = 6
WW = 12


def passed_along(value, axis, by):
    devices = 8 if axis == LAT else 32
    return lax.ppermute(value, axis, [(i, (i + by) % devices) for i in range(devices)])


def to_windows(field):
    height, breadth, features = field.shape
    blocks = field.reshape(height // WL, WL, breadth // WW, WW, features)
    return blocks.transpose(0, 2, 1, 3, 4).reshape(-1, WL * WW, features)


def from_windows(stacked, height, breadth):
    features = stacked.shape[-1]
    blocks = stacked.reshape(height // WL, breadth // WW, WL, WW, features)
    return blocks.transpose(0, 2, 1, 3, 4).reshape(height, breadth, features)


def lon_ahead(block_in):
    arrived = passed_along(block_in[:, : WW // 2], LON, -1)
    return jnp.concatenate([block_in[:, WW // 2 :], arrived], axis=1)


def lat_ahead(block_in):
    arrived = passed_along(block_in[: WL // 2], LAT, -1)
    return jnp.concatenate([block_in[WL // 2 :], arrived], axis=0)


def lon_behind(block_in):
    arrived = passed_along(block_in[:, -(WW // 2) :], LON, 1)
    return jnp.concatenate([arrived, block_in[:, : -(WW // 2)]], axis=1)


def lat_behind(block_in):
    arrived = passed_along(block_in[-(WL // 2) :], LAT, 1)
    return jnp.concatenate([arrived, block_in[: -(WL // 2)]], axis=0)


def shift_ahead(block_in):
    return lat_ahead(lon_ahead(block_in))


def shift_behind(block_in):
    return lat_behind(lon_behind(block_in))


def flat_perm(mesh_ids):
    return [(i, int(j)) for i, j in enumerate(mesh_ids)]


def core_swap():
    return flat_perm([i ^ 1 for i in range(256)])


def z_swap(bit):
    return flat_perm([i ^ (2 * bit) for i in range(256)])


def sum_grads(grad_items):
    grad_qkv, grad_out, grad_gain = grad_items
    strips = jnp.concatenate([grad_qkv, grad_out], axis=1).astype(jnp.bfloat16)
    strips = strips.reshape(512, 16, 128).transpose(1, 0, 2).reshape(8192, 128)
    core = lax.axis_index("c")
    mine = lax.dynamic_slice_in_dim(strips, core * 4096, 4096, 0)
    other = lax.dynamic_slice_in_dim(strips, (1 - core) * 4096, 4096, 0)
    arrived = lax.ppermute(other, ALL, core_swap())
    half = (mine.astype(jnp.float32) + arrived.astype(jnp.float32)).astype(jnp.bfloat16)
    gain = jnp.pad(grad_gain.reshape(4, 128), ((0, 12), (0, 0))).astype(jnp.bfloat16)
    gain_in = lax.ppermute(gain, ALL, core_swap())
    gain = (gain.astype(jnp.float32) + gain_in.astype(jnp.float32)).astype(jnp.bfloat16)
    chunks = jnp.concatenate(
        [half.reshape(16, 256, 128), jnp.broadcast_to(gain, (16, 16, 128))], axis=1
    )
    pieces = lax.all_to_all(chunks, ("x", "yh", "yl"), 0, 0, tiled=True)
    total = jnp.sum(pieces.astype(jnp.float32), axis=0).astype(jnp.bfloat16)
    for bit in (1, 2, 4):
        arrived = lax.ppermute(total, ALL, z_swap(bit))
        total = (total.astype(jnp.float32) + arrived.astype(jnp.float32)).astype(jnp.bfloat16)
    spread = jnp.broadcast_to(total, (16, 272, 128))
    half = lax.all_to_all(spread, ("x", "yh", "yl"), 0, 0, tiled=True)
    arrived = lax.ppermute(half, ALL, core_swap())
    low = jnp.where(core == 0, half, arrived)
    high = jnp.where(core == 0, arrived, half)
    grad_gain = low[0, 256:260].reshape(512).astype(jnp.float32)
    whole = jnp.concatenate([low[:, :256], high[:, :256]], axis=0).reshape(16, 512, 128)
    whole = whole.transpose(1, 0, 2).reshape(512, 2048).astype(jnp.float32)
    return whole[:, :1536], whole[:, 1536:], grad_gain


def attend(packed, d_context, region):
    win_count, win_size, _ = packed.shape
    parts = packed.reshape(win_count, win_size, 3, HEADS, HS)
    queries = parts[:, :, 0]
    key_rows = parts[:, :, 1]
    values = parts[:, :, 2]
    scaling = HS ** (-0.5)
    scores = (
        jnp.einsum("bqhd,bkhd->bhqk", queries, key_rows, preferred_element_type=jnp.float32)
        * scaling
    )
    allowed = (region[:, :, None] == region[:, None, :])[:, None]
    masked = jnp.where(allowed, scores, -1e30)
    row_max = jnp.max(masked, axis=-1, keepdims=True)
    expo_terms = jnp.exp(masked - row_max)
    probs = expo_terms / jnp.sum(expo_terms, axis=-1, keepdims=True)
    weights = probs.astype(jnp.bfloat16)
    context = jnp.einsum(
        "bhqk,bkhd->bqhd", weights, values, preferred_element_type=jnp.float32
    ).astype(jnp.bfloat16)
    context = context.reshape(win_count, win_size, HEADS * HS)
    grad_ctx = d_context.reshape(win_count, win_size, HEADS, HS)
    d_weights = jnp.einsum("bqhd,bkhd->bhqk", grad_ctx, values, preferred_element_type=jnp.float32)
    d_values = jnp.einsum(
        "bhqk,bqhd->bkhd", weights, grad_ctx, preferred_element_type=jnp.float32
    ).astype(jnp.bfloat16)
    d_scores = probs * (d_weights - jnp.sum(d_weights * probs, axis=-1, keepdims=True))
    d_scaled = (d_scores * scaling).astype(jnp.bfloat16)
    d_queries = jnp.einsum(
        "bhqk,bkhd->bqhd", d_scaled, key_rows, preferred_element_type=jnp.float32
    ).astype(jnp.bfloat16)
    d_key_rows = jnp.einsum(
        "bhqk,bqhd->bkhd", d_scaled, queries, preferred_element_type=jnp.float32
    ).astype(jnp.bfloat16)
    d_packed = jnp.stack([d_queries, d_key_rows, d_values], axis=2)
    return (context, d_packed.reshape(win_count, win_size, 3 * HEADS * HS))


def local(latent, norm_gain, w_qkv, w_out, cotangent):
    height, breadth, features = latent.shape
    tokens_dev = height * breadth
    latent_f = latent.astype(jnp.float32)
    centred = latent_f - jnp.mean(latent_f, axis=-1, keepdims=True)
    variance = jnp.mean(centred * centred, axis=-1, keepdims=True)
    recip_std = lax.rsqrt(variance + 1e-05)
    normed = centred * recip_std
    scaled_in = (normed * norm_gain).astype(jnp.bfloat16)
    shifted_in = shift_ahead(scaled_in)
    shifted_cot = shift_ahead(cotangent)
    last_row = lax.axis_index(LAT) == 7
    wrapped = jnp.logical_and(last_row, jnp.arange(height) >= height - WL // 2).astype(jnp.int32)
    region_grid = jnp.broadcast_to(wrapped[:, None, None], (height, breadth, 1))
    region_win = to_windows(region_grid)[:, :, 0]
    flat_in = shifted_in.reshape(tokens_dev, features)
    flat_cot = shifted_cot.reshape(tokens_dev, features)
    packed = jnp.dot(flat_in, w_qkv, preferred_element_type=jnp.float32).astype(jnp.bfloat16)
    d_context = jnp.einsum("te,de->td", flat_cot, w_out, preferred_element_type=jnp.float32).astype(
        jnp.bfloat16
    )
    context_w, d_packed_w = attend(
        to_windows(packed.reshape(height, breadth, 3 * features)),
        to_windows(d_context.reshape(height, breadth, features)),
        region_win,
    )
    context_flat = from_windows(context_w, height, breadth).reshape(tokens_dev, features)
    attn_out = jnp.dot(context_flat, w_out, preferred_element_type=jnp.float32).astype(jnp.bfloat16)
    grad_out = jnp.einsum("td,te->de", context_flat, flat_cot, preferred_element_type=jnp.float32)
    d_packed_flat = from_windows(d_packed_w, height, breadth).reshape(tokens_dev, 3 * features)
    grad_qkv = jnp.einsum("td,tf->df", flat_in, d_packed_flat, preferred_element_type=jnp.float32)
    d_shifted = jnp.einsum(
        "tf,df->td", d_packed_flat, w_qkv, preferred_element_type=jnp.float32
    ).astype(jnp.bfloat16)
    attn_moved = shift_behind(attn_out.reshape(height, breadth, features))
    d_moved = shift_behind(d_shifted.reshape(height, breadth, features)).astype(jnp.float32)
    mixed = (latent_f + attn_moved.astype(jnp.float32)).astype(jnp.bfloat16)
    grad_gain = jnp.sum(d_moved * normed, axis=(0, 1))
    hidden_grad = d_moved * norm_gain
    d_norm_part = recip_std * (
        hidden_grad
        - jnp.mean(hidden_grad, axis=-1, keepdims=True)
        - normed * jnp.mean(hidden_grad * normed, axis=-1, keepdims=True)
    )
    d_latent = (cotangent.astype(jnp.float32) + d_norm_part).astype(jnp.bfloat16)
    grad_qkv, grad_out, grad_gain = sum_grads((grad_qkv, grad_out, grad_gain))
    return (mixed, d_latent, grad_qkv, grad_out, grad_gain)


def solution(mesh):
    fine = Mesh(mesh.devices.reshape(4, 2, 2, 8, 2), ALL)
    in_specs = (P(LAT, LON, None), P(), P(), P(), P(LAT, LON, None))
    out_specs = (P(LAT, LON, None), P(LAT, LON, None), P(), P(), P())
    return jax.shard_map(local, mesh=fine, in_specs=in_specs, out_specs=out_specs, check_vma=False)
```

```python
import functools

import jax
import jax.numpy as jnp
import numpy as np
from jax import lax
from jax.experimental import pallas as pl
from jax.experimental.pallas import tpu as pltpu
from jax.sharding import Mesh, PartitionSpec as P

ALL = ("x", "yh", "yl", "z", "c")
LAT = ("x", "yh")
LON = ("yl", "z", "c")
PLANE = ("x", "yh", "yl")
HEADS = 16
HS = 32
WL = 6
WW = 12
TILE = (6, 48)
D = 512
WINDOWS = 4
ROWS = 80
TOKENS = WINDOWS * ROWS
GROUP = 8
SPAN = GROUP * HS
EDGE = 16
HALF = 3 * TILE[1]
EDGES = 3 * EDGE
STRIP = 512 * 8
CHUNK = STRIP // 16
f32 = jnp.float32
bf16 = jnp.bfloat16
NT = (((1,), (1,)), ((), ()))
TN = (((0,), (0,)), ((), ()))


def gather_matrix():
    picks = np.zeros((TOKENS, 2 * HALF + 2 * EDGES), np.float32)
    for w in range(WINDOWS):
        for r in range(WL):
            for c in range(WW):
                col = w * WW + c + WW // 2
                below = r >= WL // 2
                line = r - WL // 2 if below else r
                if col < TILE[1]:
                    at = line * TILE[1] + col + (HALF if below else 0)
                else:
                    at = 2 * HALF + line * EDGE + col - TILE[1] + (EDGES if below else 0)
                picks[w * ROWS + r * WW + c, at] = 1.0
    return picks.astype(jnp.bfloat16)


def dot(a, b, dims=(((1,), (0,)), ((), ()))):
    return lax.dot_general(a, b, dims, preferred_element_type=f32)


def block_kernel(
    where_am_i,
    lat_ref, cot_ref, halo_lat_ref, halo_lon_ref, halo_cor_ref, gain_ref, w_qkv_ref, w_out_ref, picks_ref,
    own_ref, back_lat_ref, back_lon_ref, back_cor_ref, mine_ref, other_ref,
    scaled_s, normed_s, packed_s, dctx_s, ctx_s, dpacked_s, cot_s, latent_s,
):
    last_lat, core = where_am_i()
    picks = picks_ref[...]

    def gather(own, at):
        stack = jnp.concatenate(
            [own[HALF:, :], halo_lat_ref[at], halo_lon_ref[at], halo_cor_ref[at]], axis=0
        )
        return dot(picks, stack)

    latent = gather(lat_ref, 0)
    latent_s[...] = latent
    cot_s[...] = gather(cot_ref, 1).astype(bf16)
    centred = latent - jnp.mean(latent, axis=-1, keepdims=True)
    variance = jnp.mean(centred * centred, axis=-1, keepdims=True)
    recip_std = lax.rsqrt(variance + 1e-05)
    normed = centred * recip_std
    normed_s[...] = normed
    scaled_s[...] = (normed * gain_ref[...]).astype(bf16)
    packed_s[...] = dot(scaled_s[...], w_qkv_ref[...]).astype(bf16)
    dctx_s[...] = dot(cot_s[...], w_out_ref[...], NT).astype(bf16)

    scaling = HS ** (-0.5)
    key_at = lax.broadcasted_iota(jnp.int32, (ROWS, GROUP * ROWS), 0)
    lane = lax.broadcasted_iota(jnp.int32, (1, GROUP * ROWS), 1)
    query_at = lane
    for h in range(1, GROUP):
        query_at = query_at - jnp.where(lane >= h * ROWS, ROWS, 0)
    split = WL // 2 * WW
    differ = jnp.logical_and(last_lat, (key_at >= split) != (query_at >= split))
    excluded = jnp.logical_or(key_at >= WL * WW, differ)
    bias = jnp.where(excluded, -1e30, 0.0).astype(f32)
    head_of = lax.broadcasted_iota(jnp.int32, (GROUP, 1, SPAN), 2) // HS
    head = lax.broadcasted_iota(jnp.int32, (GROUP, 1, SPAN), 0)
    own_head = jnp.where(head_of == head, 1.0, 0.0).astype(f32)
    own_head_b = own_head.astype(bf16)

    def spread(rows):
        return (rows[None] * own_head_b).reshape(GROUP * ROWS, SPAN)

    def collect(rows):
        return jnp.sum(rows.reshape(GROUP, ROWS, SPAN) * own_head, axis=0).astype(bf16)

    for w in range(WINDOWS):
        for g in range(HEADS // GROUP):
            rows = slice(w * ROWS, (w + 1) * ROWS)
            at = [slice(b * D + g * SPAN, b * D + (g + 1) * SPAN) for b in range(3)]
            keys = packed_s[rows, at[1]]
            values = packed_s[rows, at[2]]
            queries = spread(packed_s[rows, at[0]])
            d_context = spread(dctx_s[rows, at[0]])
            scores = dot(keys, queries, NT) * (scaling * 1.4426950408889634) + bias
            expo = jnp.exp2(scores - jnp.max(scores, axis=0, keepdims=True))
            probs = expo * (1.0 / jnp.sum(expo, axis=0, keepdims=True))
            weights = probs.astype(bf16)
            d_weights = dot(values, d_context, NT)
            mean_d = jnp.sum(d_weights * probs, axis=0, keepdims=True)
            d_scaled = ((probs * scaling) * (d_weights - mean_d)).astype(bf16)
            ctx_s[rows, at[0]] = collect(dot(weights, values, TN))
            dpacked_s[rows, at[2]] = dot(weights, d_context).astype(bf16)
            dpacked_s[rows, at[0]] = collect(dot(d_scaled, keys, TN))
            dpacked_s[rows, at[1]] = dot(d_scaled, queries).astype(bf16)

    first = core == 0
    for strip in range(0, 8, 2):
        cols = slice(strip * 128, strip * 128 + 256)
        low = dot(scaled_s[...], dpacked_s[:, cols], TN)
        if strip < 4:
            high = dot(scaled_s[...], dpacked_s[:, 2 * D + strip * 128 : 2 * D + strip * 128 + 256], TN)
        else:
            high = dot(ctx_s[...], cot_s[:, strip * 128 - D : strip * 128 - D + 256], TN)
        keep = jnp.where(first, low, high).astype(bf16)
        give = jnp.where(first, high, low).astype(bf16)
        for k in range(2):
            to = slice((strip + k) * 512, (strip + k + 1) * 512)
            mine_ref[to, :] = keep[:, k * 128 : (k + 1) * 128]
            other_ref[to, :] = give[:, k * 128 : (k + 1) * 128]

    normed = normed_s[...]
    d_shifted = dot(dpacked_s[...], w_qkv_ref[...], NT).astype(bf16).astype(f32)
    grad_gain = jnp.sum(d_shifted * normed, axis=0, keepdims=True)
    gain_rows = jnp.concatenate(
        [grad_gain[:, k * 128 : (k + 1) * 128] for k in range(4)] + [jnp.zeros((12, 128), f32)], axis=0
    ).astype(bf16)
    mine_ref[STRIP:, :] = gain_rows
    other_ref[STRIP:, :] = gain_rows
    hidden = d_shifted * gain_ref[...]
    part = recip_std * (
        hidden
        - jnp.mean(hidden, axis=-1, keepdims=True)
        - normed * jnp.mean(hidden * normed, axis=-1, keepdims=True)
    )
    d_latent = (cot_s[...].astype(f32) + part).astype(bf16)
    attn = dot(ctx_s[...], w_out_ref[...]).astype(bf16).astype(f32)
    mixed = (latent_s[...] + attn).astype(bf16)
    for k, value in enumerate((mixed, d_latent)):
        moved = dot(picks, value, TN).astype(bf16)
        own_ref[k] = moved[:HALF]
        back_lat_ref[k] = moved[HALF : 2 * HALF]
        back_lon_ref[k] = moved[2 * HALF : 2 * HALF + EDGES]
        back_cor_ref[k] = moved[2 * HALF + EDGES :]


def here():
    return jnp.logical_and(lax.axis_index("x") == 3, lax.axis_index("yh") == 1), lax.axis_index("c")


def vmem_call(kernel, out_shapes, scratch, flops, moved, count):
    whole = pl.BlockSpec(memory_space=pltpu.VMEM)
    return pl.pallas_call(
        kernel,
        out_shape=out_shapes,
        in_specs=[whole] * count,
        out_specs=[whole] * len(out_shapes),
        scratch_shapes=scratch,
        compiler_params=pltpu.CompilerParams(vmem_limit_bytes=40 * 1024 * 1024),
        cost_estimate=pl.CostEstimate(flops=flops, bytes_accessed=moved, transcendentals=0),
    )


def shape(*dims, dtype=bf16):
    return jax.ShapeDtypeStruct(dims, dtype)


def block(where_am_i, latent, cot, halo_lat, halo_lon, halo_cor, gain, w_qkv, w_out):
    return vmem_call(
        functools.partial(block_kernel, where_am_i),
        [
            shape(2, HALF, D), shape(2, HALF, D), shape(2, EDGES, D), shape(2, EDGES, D),
            shape(STRIP + 16, 128), shape(STRIP + 16, 128),
        ],
        [
            pltpu.VMEM((TOKENS, D), bf16), pltpu.VMEM((TOKENS, D), f32), pltpu.VMEM((TOKENS, 3 * D), bf16),
            pltpu.VMEM((TOKENS, D), bf16), pltpu.VMEM((TOKENS, D), bf16), pltpu.VMEM((TOKENS, 3 * D), bf16),
            pltpu.VMEM((TOKENS, D), bf16), pltpu.VMEM((TOKENS, D), f32),
        ],
        6_000_000_000, 8_000_000, 9,
    )(latent, cot, halo_lat, halo_lon, halo_cor, gain, w_qkv, w_out, jnp.asarray(gather_matrix()))


def add_kernel(mine_ref, arrived_ref, chunks_ref):
    gain = (mine_ref[STRIP:, :].astype(f32) + arrived_ref[STRIP:, :].astype(f32)).astype(bf16)
    for k in range(16):
        at = slice(k * CHUNK, (k + 1) * CHUNK)
        chunks_ref[k, :CHUNK] = (mine_ref[at, :].astype(f32) + arrived_ref[at, :].astype(f32)).astype(bf16)
        chunks_ref[k, CHUNK:] = gain


def unpack_kernel(where_am_i, half_ref, arrived_ref, qkv_ref, out_ref, gain_ref):
    first = where_am_i()[1] == 0
    for k in range(16):
        ours = half_ref[k, :CHUNK].astype(f32)
        theirs = arrived_ref[k, :CHUNK].astype(f32)
        low = jnp.where(first, ours, theirs)
        high = jnp.where(first, theirs, ours)
        strip, rows = k // 2, slice(k % 2 * CHUNK, (k % 2 + 1) * CHUNK)
        qkv_ref[rows, strip * 128 : (strip + 1) * 128] = low
        if strip < 4:
            qkv_ref[rows, 2 * D + strip * 128 : 2 * D + (strip + 1) * 128] = high
        else:
            out_ref[rows, strip * 128 - D : (strip + 1) * 128 - D] = high
    gain = jnp.where(first, half_ref[0, CHUNK:].astype(f32), arrived_ref[0, CHUNK:].astype(f32))
    for k in range(4):
        gain_ref[:, k * 128 : (k + 1) * 128] = gain[k : k + 1, :]


def place_kernel(own_ref, lat_ref, lon_ref, cor_ref, mixed_ref, d_latent_ref):
    for k, out_ref in enumerate((mixed_ref, d_latent_ref)):
        for r in range(3):
            for first, body_ref, edge_ref in ((0, lat_ref, cor_ref), (HALF, own_ref, lon_ref)):
                at = r * TILE[1]
                edge = edge_ref[k, r * EDGE : (r + 1) * EDGE].astype(f32)
                body = body_ref[k, at : at + EDGE].astype(f32)
                out_ref[first + at : first + at + EDGE, :] = (body + edge).astype(bf16)
                out_ref[first + at + EDGE : first + at + TILE[1], :] = body_ref[k, at + EDGE : at + TILE[1]]


def shifted(lat_by, lon_by):
    pairs = []
    for i in range(256):
        lat, lon = i // 32, i % 32
        pairs.append((i, (lat + lat_by) % 8 * 32 + (lon + lon_by) % 32))
    return pairs


def swapped(bits):
    return [(i, i ^ bits) for i in range(256)]


def send(value, pairs):
    return lax.ppermute(value, ALL, pairs)


def sum_grads(mine, other):
    arrived = send(other, swapped(1))
    chunks = vmem_call(add_kernel, [shape(16, CHUNK + 16, 128)], [], 1_000_000, 4_000_000, 2)(mine, arrived)[0]
    pieces = lax.all_to_all(chunks, PLANE, 0, 0, tiled=True)
    total = jnp.sum(pieces.astype(f32), axis=0).astype(bf16)
    for bit in (2, 4, 8):
        total = (total.astype(f32) + send(total, swapped(bit)).astype(f32)).astype(bf16)
    spread = jnp.broadcast_to(total, (16, CHUNK + 16, 128))
    half = lax.all_to_all(spread, PLANE, 0, 0, tiled=True)
    arrived = send(half, swapped(1))
    grad_qkv, grad_out, grad_gain = vmem_call(
        functools.partial(unpack_kernel, here),
        [shape(D, 3 * D, dtype=f32), shape(D, D, dtype=f32), shape(1, D, dtype=f32)],
        [], 1_000_000, 6_000_000, 2,
    )(half, arrived)
    return grad_qkv, grad_out, grad_gain.reshape(D)


def local(latent, norm_gain, w_qkv, w_out, cotangent):
    both = jnp.stack([latent[:3], cotangent[:3]])
    halo_lat = send(both.reshape(2, HALF, D), shifted(-1, 0))
    halo_cor = send(both[:, :, :EDGE].reshape(2, EDGES, D), shifted(-1, -1))
    edge = jnp.stack([latent[3:, :EDGE], cotangent[3:, :EDGE]])
    halo_lon = send(edge.reshape(2, EDGES, D), shifted(0, -1))
    own, back_lat, back_lon, back_cor, mine, other = block(
        here, latent.reshape(-1, D), cotangent.reshape(-1, D), halo_lat, halo_lon, halo_cor,
        norm_gain.reshape(1, D), w_qkv, w_out,
    )
    grad_qkv, grad_out, grad_gain = sum_grads(mine, other)
    came_lat = send(back_lat, shifted(1, 0))
    came_lon = send(back_lon, shifted(0, 1))
    came_cor = send(back_cor, shifted(1, 1))
    mixed, d_latent = vmem_call(
        place_kernel, [shape(2 * HALF, D), shape(2 * HALF, D)], [], 1_000_000, 2_000_000, 4
    )(own, came_lat, came_lon, came_cor)
    return mixed.reshape(*TILE, D), d_latent.reshape(*TILE, D), grad_qkv, grad_out, grad_gain


def solution(mesh):
    fine = Mesh(mesh.devices.reshape(4, 2, 2, 8, 2), ALL)
    in_specs = (P(LAT, LON, None), P(), P(), P(), P(LAT, LON, None))
    out_specs = (P(LAT, LON, None), P(LAT, LON, None), P(), P(), P())
    return jax.shard_map(local, mesh=fine, in_specs=in_specs, out_specs=out_specs, check_vma=False)
```

```python
import functools

import jax
import jax.numpy as jnp
from jax import lax
from jax.experimental import pallas as pl
from jax.experimental.pallas import tpu as pltpu
from jax.sharding import Mesh, PartitionSpec as P

ALL = ("x", "yh", "yl", "z", "c")
LAT = ("x", "yh")
LON = ("yl", "z", "c")
PLANE = ("x", "yh", "yl")
HEADS = 16
HS = 32
WL = 6
WW = 12
TILE = (6, 48)
D = 512
WINDOWS = 4
ROWS = 80
TOKENS = WINDOWS * ROWS
GROUP = 8
SPAN = GROUP * HS
EDGE = 16
HALF = 3 * TILE[1]
EDGES = 3 * EDGE
STRIP = 512 * 8
CHUNK = STRIP // 16
SUMMED = CHUNK + 16
BACK = HALF + EDGES
f32 = jnp.float32
bf16 = jnp.bfloat16
NT = (((1,), (1,)), ((), ()))
TN = (((0,), (0,)), ((), ()))


def dot(a, b, dims=(((1,), (0,)), ((), ()))):
    return lax.dot_general(a, b, dims, preferred_element_type=f32)


def norm(latent):
    centred = latent - jnp.mean(latent, axis=-1, keepdims=True)
    variance = jnp.mean(centred * centred, axis=-1, keepdims=True)
    recip_std = lax.rsqrt(variance + 1e-05)
    return centred * recip_std, recip_std


def picks_kernel(w_out_ref, picks_ref, w_out_s):
    w_out_s[...] = w_out_ref[...]
    def count(value, step, upto):
        return sum(jnp.where(value >= step * k, 1, 0) for k in range(1, upto))

    row = lax.broadcasted_iota(jnp.int32, (TOKENS, 128), 0)
    window = count(row, ROWS, WINDOWS)
    cell = row - window * ROWS
    line = count(cell, WW, WL)
    col = (window + 0) * WW + cell - line * WW + WW // 2
    below = line >= WL // 2
    line = jnp.where(below, line - WL // 2, line)
    inside = line * TILE[1] + col + jnp.where(below, HALF, 0)
    beyond = 2 * HALF + line * EDGE + col - TILE[1] + jnp.where(below, EDGES, 0)
    at = jnp.where(col < TILE[1], inside, beyond)
    at = jnp.where(cell < WL * WW, at, -1)
    lane = lax.broadcasted_iota(jnp.int32, (TOKENS, 128), 1)
    for k in range(3):
        picks_ref[:, k * 128 : (k + 1) * 128] = jnp.where(at == lane + k * 128, 1.0, 0.0).astype(bf16)


def attend_kernel(
    where_am_i,
    lat_ref, cot_ref, halo_lat_ref, halo_lon_ref, halo_cor_ref, gain_ref, w_qkv_ref, w_out_ref, picks_ref,
    mine_ref, other_ref, latent_s, cot_s, ctx_s, dpacked_s,
    scaled_s, packed_s, dctx_s,
):
    last_lat, core = where_am_i()
    picks = picks_ref[...]

    def gather(own, at):
        stack = jnp.concatenate(
            [own[HALF:, :], halo_lat_ref[at], halo_lon_ref[at], halo_cor_ref[at]], axis=0
        )
        return dot(picks, stack)

    latent = gather(lat_ref, 0)
    latent_s[...] = latent.astype(bf16)
    cot_s[...] = gather(cot_ref, 1).astype(bf16)
    normed, _ = norm(latent)
    scaled_s[...] = (normed * gain_ref[...]).astype(bf16)
    packed_s[...] = dot(scaled_s[...], w_qkv_ref[...]).astype(bf16)
    dctx_s[...] = dot(cot_s[...], w_out_ref[...], NT).astype(bf16)

    scaling = HS ** (-0.5)
    key_at = lax.broadcasted_iota(jnp.int32, (ROWS, GROUP * ROWS), 0)
    lane = lax.broadcasted_iota(jnp.int32, (1, GROUP * ROWS), 1)
    query_at = lane
    for h in range(1, GROUP):
        query_at = query_at - jnp.where(lane >= h * ROWS, ROWS, 0)
    split = WL // 2 * WW
    differ = jnp.logical_and(last_lat, (key_at >= split) != (query_at >= split))
    excluded = jnp.logical_or(key_at >= WL * WW, differ)
    bias = jnp.where(excluded, -1e30, 0.0).astype(f32)
    head_of = lax.broadcasted_iota(jnp.int32, (GROUP, 1, SPAN), 2) // HS
    head = lax.broadcasted_iota(jnp.int32, (GROUP, 1, SPAN), 0)
    own_head = jnp.where(head_of == head, 1.0, 0.0).astype(f32)
    own_head_b = own_head.astype(bf16)

    def spread(rows):
        return (rows[None] * own_head_b).reshape(GROUP * ROWS, SPAN)

    def collect(rows):
        return jnp.sum(rows.reshape(GROUP, ROWS, SPAN) * own_head, axis=0).astype(bf16)

    for w in range(WINDOWS):
        for g in range(HEADS // GROUP):
            rows = slice(w * ROWS, (w + 1) * ROWS)
            at = [slice(b * D + g * SPAN, b * D + (g + 1) * SPAN) for b in range(3)]
            keys = packed_s[rows, at[1]]
            values = packed_s[rows, at[2]]
            queries = spread(packed_s[rows, at[0]])
            d_context = spread(dctx_s[rows, at[0]])
            scores = dot(keys, queries, NT) * (scaling * 1.4426950408889634) + bias
            expo = jnp.exp2(scores - jnp.max(scores, axis=0, keepdims=True))
            probs = expo * (1.0 / jnp.sum(expo, axis=0, keepdims=True))
            weights = probs.astype(bf16)
            d_weights = dot(values, d_context, NT)
            mean_d = jnp.sum(d_weights * probs, axis=0, keepdims=True)
            d_scaled = ((probs * scaling) * (d_weights - mean_d)).astype(bf16)
            ctx_s[rows, at[0]] = collect(dot(weights, values, TN))
            dpacked_s[rows, at[2]] = dot(weights, d_context).astype(bf16)
            dpacked_s[rows, at[0]] = collect(dot(d_scaled, keys, TN))
            dpacked_s[rows, at[1]] = dot(d_scaled, queries).astype(bf16)

    first = core == 0
    for strip in range(0, 8, 2):
        cols = slice(strip * 128, strip * 128 + 256)
        low = dot(scaled_s[...], dpacked_s[:, cols], TN)
        if strip < 4:
            high = dot(scaled_s[...], dpacked_s[:, 2 * D + strip * 128 : 2 * D + strip * 128 + 256], TN)
        else:
            high = dot(ctx_s[...], cot_s[:, strip * 128 - D : strip * 128 - D + 256], TN)
        keep = jnp.where(first, low, high).astype(bf16)
        give = jnp.where(first, high, low).astype(bf16)
        for k in range(2):
            to = slice((strip + k) * 512, (strip + k + 1) * 512)
            mine_ref[to, :] = keep[:, k * 128 : (k + 1) * 128]
            other_ref[to, :] = give[:, k * 128 : (k + 1) * 128]


def finish_kernel(
    latent_ref, cot_ref, ctx_ref, dpacked_ref, gain_ref, w_qkv_ref, w_out_ref, picks_ref,
    own_ref, back_ref, back_lon_ref, gain_rows_ref,
):
    latent = latent_ref[...].astype(f32)
    normed, recip_std = norm(latent)
    d_shifted = dot(dpacked_ref[...], w_qkv_ref[...], NT).astype(bf16).astype(f32)
    grad_gain = jnp.sum(d_shifted * normed, axis=0, keepdims=True)
    gain_rows_ref[...] = jnp.concatenate(
        [grad_gain[:, k * 128 : (k + 1) * 128] for k in range(4)] + [jnp.zeros((12, 128), f32)], axis=0
    ).astype(bf16)
    hidden = d_shifted * gain_ref[...]
    part = recip_std * (
        hidden
        - jnp.mean(hidden, axis=-1, keepdims=True)
        - normed * jnp.mean(hidden * normed, axis=-1, keepdims=True)
    )
    d_latent = (cot_ref[...].astype(f32) + part).astype(bf16)
    attn = dot(ctx_ref[...], w_out_ref[...]).astype(bf16).astype(f32)
    mixed = (latent + attn).astype(bf16)
    picks = picks_ref[...]
    for k, value in enumerate((mixed, d_latent)):
        moved = dot(picks, value, TN).astype(bf16)
        own_ref[k] = moved[:HALF]
        back_ref[k, :HALF] = moved[HALF : 2 * HALF]
        back_ref[k, HALF:] = moved[2 * HALF + EDGES :]
        back_lon_ref[k] = moved[2 * HALF : 2 * HALF + EDGES]


def here():
    return jnp.logical_and(lax.axis_index("x") == 3, lax.axis_index("yh") == 1), lax.axis_index("c")


def vmem_call(kernel, out_shapes, scratch, flops, moved, count):
    whole = pl.BlockSpec(memory_space=pltpu.VMEM)
    return pl.pallas_call(
        kernel,
        out_shape=out_shapes,
        in_specs=[whole] * count,
        out_specs=[whole] * len(out_shapes),
        scratch_shapes=scratch,
        compiler_params=pltpu.CompilerParams(vmem_limit_bytes=40 * 1024 * 1024),
        cost_estimate=pl.CostEstimate(flops=flops, bytes_accessed=moved, transcendentals=0),
    )


def shape(*dims, dtype=bf16):
    return jax.ShapeDtypeStruct(dims, dtype)


def block(where_am_i, latent, cot, halo_lat, halo_lon, halo_cor, gain, w_qkv, w_out):
    picks, w_out = vmem_call(picks_kernel, [shape(TOKENS, 384), shape(D, D)], [], 1_000_000, 500_000, 1)(w_out)
    mine, other, latent_w, cot_w, ctx, dpacked = vmem_call(
        functools.partial(attend_kernel, where_am_i),
        [
            shape(STRIP, 128), shape(STRIP, 128),
            shape(TOKENS, D), shape(TOKENS, D), shape(TOKENS, D), shape(TOKENS, 3 * D),
        ],
        [
            pltpu.VMEM((TOKENS, D), bf16), pltpu.VMEM((TOKENS, 3 * D), bf16), pltpu.VMEM((TOKENS, D), bf16),
        ],
        5_000_000_000, 8_000_000, 9,
    )(latent, cot, halo_lat, halo_lon, halo_cor, gain, w_qkv, w_out, picks)
    own, back, back_lon, gain_rows = vmem_call(
        finish_kernel,
        [shape(2, HALF, D), shape(2, BACK, D), shape(2, EDGES, D), shape(16, 128)],
        [], 1_500_000_000, 4_000_000, 8,
    )(latent_w, cot_w, ctx, dpacked, gain, w_qkv, w_out, picks)
    return own, back, back_lon, mine, other, gain_rows


def add_kernel(mine_ref, arrived_ref, gain_ref, chunks_ref):
    for k in range(16):
        at = slice(k * CHUNK, (k + 1) * CHUNK)
        chunks_ref[k, :CHUNK] = (mine_ref[at, :].astype(f32) + arrived_ref[at, :].astype(f32)).astype(bf16)
        chunks_ref[k, CHUNK:] = gain_ref[...]


def spread_kernel(total_ref, arrived_ref, came_ref, back_lon_ref, spread_ref, edge_ref):
    total = (total_ref[...].astype(f32) + arrived_ref[...].astype(f32)).astype(bf16)
    for k in range(16):
        spread_ref[k] = total
    for k in range(2):
        edge_ref[k, :EDGES] = back_lon_ref[k]
        edge_ref[k, EDGES:] = came_ref[k, HALF:]


def unpack_kernel(where_am_i, side, half_ref, *refs):
    qkv_ref, out_ref = refs[-4 - side], refs[-3 - side]
    wide_s, sems = refs[-2:]
    core = where_am_i()[1]
    low = core == side

    def store(start):
        for block in range(4):
            cols = slice(block * 256, (block + 1) * 256)
            if start:
                for k in range(4 * block, 4 * block + 4):
                    at = slice(k // 2 * 128, (k // 2 + 1) * 128)
                    wide_s[k % 2 * CHUNK : (k % 2 + 1) * CHUNK, at] = half_ref[k, :CHUNK].astype(f32)

            def copy(ref, first):
                to = ref.at[:, first : first + 256]
                move = pltpu.make_async_copy(wide_s.at[:, cols], to, sems.at[block])
                move.start() if start else move.wait()

            pl.when(low)(lambda: copy(qkv_ref, block * 256))
            if block < 2:
                pl.when(jnp.logical_not(low))(lambda: copy(qkv_ref, 2 * D + block * 256))
            else:
                pl.when(jnp.logical_not(low))(lambda: copy(out_ref, block * 256 - D))

    store(True)
    if side:
        own_ref, gain_ref = refs[0], refs[-3]
        gain = half_ref[0, CHUNK:].astype(f32) + own_ref[0, CHUNK:].astype(f32)
        for k in range(4):
            gain_ref[:, k * 128 : (k + 1) * 128] = gain[k : k + 1, :]
    store(False)


def unpack(where_am_i, side, half, *rest):
    whole = pl.BlockSpec(memory_space=pltpu.VMEM)
    stay = pl.BlockSpec(memory_space=pltpu.HBM)
    outs = [shape(D, 3 * D, dtype=f32), shape(D, D, dtype=f32)]
    return pl.pallas_call(
        functools.partial(unpack_kernel, where_am_i, side),
        out_shape=outs + [shape(1, D, dtype=f32)] * side,
        in_specs=[whole] + [whole, stay, stay] * side,
        out_specs=[stay, stay] + [whole] * side,
        scratch_shapes=[pltpu.VMEM((D, 2 * D), f32), pltpu.SemaphoreType.DMA((4,))],
        input_output_aliases={2: 0, 3: 1} if side else {},
        compiler_params=pltpu.CompilerParams(vmem_limit_bytes=40 * 1024 * 1024),
        cost_estimate=pl.CostEstimate(flops=1_000_000, bytes_accessed=3_000_000, transcendentals=0),
    )(half, *rest)


def place_kernel(own_ref, came_ref, edge_ref, mixed_ref, d_latent_ref):
    for k, out_ref in enumerate((mixed_ref, d_latent_ref)):
        for r in range(3):
            at = r * TILE[1]
            for first, body_ref, edges in ((0, came_ref, EDGES), (HALF, own_ref, 0)):
                edge = edge_ref[k, edges + r * EDGE : edges + (r + 1) * EDGE].astype(f32)
                body = body_ref[k, at : at + EDGE].astype(f32)
                out_ref[first + at : first + at + EDGE, :] = (body + edge).astype(bf16)
                out_ref[first + at + EDGE : first + at + TILE[1], :] = body_ref[k, at + EDGE : at + TILE[1]]


def shifted(lat_by, lon_by):
    pairs = []
    for i in range(256):
        lat, lon = i // 32, i % 32
        pairs.append((i, (lat + lat_by) % 8 * 32 + (lon + lon_by) % 32))
    return pairs


def swapped(bits):
    return [(i, i ^ bits) for i in range(256)]


def send(value, pairs):
    return lax.ppermute(value, ALL, pairs)


def sum_and_return(own, back, back_lon, mine, other, gain_rows):
    arrived = send(other, swapped(1))
    chunks = vmem_call(
        add_kernel, [shape(16, SUMMED, 128)], [], 1_000_000, 4_000_000, 3
    )(mine, arrived, gain_rows)[0]
    pieces = lax.all_to_all(chunks, PLANE, 0, 0, tiled=True)
    total = jnp.sum(pieces.astype(f32), axis=0).astype(bf16)
    for bits in (2, 4):
        total = (total.astype(f32) + send(total, swapped(bits)).astype(f32)).astype(bf16)
    spread, edge = vmem_call(
        spread_kernel, [shape(16, SUMMED, 128), shape(2, 2 * EDGES, D)], [], 1_000_000, 3_000_000, 4
    )(total, send(total, swapped(12)), came := send(back, shifted(1, 0)), back_lon)
    half = lax.all_to_all(spread, PLANE, 0, 0, tiled=True)
    edge = send(edge, shifted(0, 1))
    half, edge = lax.optimization_barrier((half, edge))
    arrived = send(half, swapped(1))
    parts = unpack(here, 0, half)
    mixed, d_latent = vmem_call(
        place_kernel, [shape(2 * HALF, D), shape(2 * HALF, D)], [], 1_000_000, 2_000_000, 3
    )(own, came, edge)
    grad_qkv, grad_out, grad_gain = unpack(here, 1, arrived, half, *parts)
    return mixed.reshape(*TILE, D), d_latent.reshape(*TILE, D), grad_qkv, grad_out, grad_gain.reshape(D)


def local(latent, norm_gain, w_qkv, w_out, cotangent):
    both = jnp.stack([latent[:3], cotangent[:3]])
    halo_lat = send(both.reshape(2, HALF, D), shifted(-1, 0))
    halo_cor = send(both[:, :, :EDGE].reshape(2, EDGES, D), shifted(-1, -1))
    edge = jnp.stack([latent[3:, :EDGE], cotangent[3:, :EDGE]])
    halo_lon = send(edge.reshape(2, EDGES, D), shifted(0, -1))
    return sum_and_return(*block(
        here, latent.reshape(-1, D), cotangent.reshape(-1, D), halo_lat, halo_lon, halo_cor,
        norm_gain.reshape(1, D), w_qkv, w_out,
    ))


def solution(mesh):
    fine = Mesh(mesh.devices.reshape(4, 2, 2, 8, 2), ALL)
    in_specs = (P(LAT, LON, None), P(), P(), P(), P(LAT, LON, None))
    out_specs = (P(LAT, LON, None), P(LAT, LON, None), P(), P(), P())
    return jax.shard_map(local, mesh=fine, in_specs=in_specs, out_specs=out_specs, check_vma=False)
```

```python
import functools

import jax
import jax.numpy as jnp
from jax import lax
from jax.experimental import pallas as pl
from jax.experimental.pallas import tpu as pltpu
from jax.sharding import Mesh, PartitionSpec as P

ALL = ("x", "yh", "yl", "z", "c")
LAT = ("x", "yh")
LON = ("yl", "z", "c")
PLANE = ("x", "yh", "yl")
HEADS = 16
HS = 32
WL = 6
WW = 12
TILE = (6, 48)
D = 512
WINDOWS = 4
ROWS = 80
TOKENS = WINDOWS * ROWS
GROUP = 8
SPAN = GROUP * HS
EDGE = 8
HALF = 3 * TILE[1]
EDGES = 3 * EDGE
STRIP = 512 * 8
CHUNK = STRIP // 16
SUMMED = CHUNK + 8
BACK = HALF + EDGES
f32 = jnp.float32
bf16 = jnp.bfloat16
NT = (((1,), (1,)), ((), ()))
TN = (((0,), (0,)), ((), ()))


def dot(a, b, dims=(((1,), (0,)), ((), ()))):
    return lax.dot_general(a, b, dims, preferred_element_type=f32)


def norm(latent):
    centred = latent - jnp.mean(latent, axis=-1, keepdims=True)
    variance = jnp.mean(centred * centred, axis=-1, keepdims=True)
    recip_std = lax.rsqrt(variance + 1e-05)
    return centred * recip_std, recip_std


def prepare_kernel(w_qkv_ref, w_out_ref, picks_ref, w_qkv_s, w_out_s):
    w_qkv_s[...] = w_qkv_ref[...]
    w_out_s[...] = w_out_ref[...]
    def count(value, step, upto):
        return sum(jnp.where(value >= step * k, 1, 0) for k in range(1, upto))

    row = lax.broadcasted_iota(jnp.int32, (TOKENS, 128), 0)
    window = count(row, ROWS, WINDOWS)
    cell = row - window * ROWS
    line = count(cell, WW, WL)
    col = (window + 0) * WW + cell - line * WW + WW // 2
    below = line >= WL // 2
    line = jnp.where(below, line - WL // 2, line)
    inside = line * TILE[1] + col + jnp.where(below, HALF, 0)
    beyond = 2 * HALF + line * EDGE + col - TILE[1] + jnp.where(below, EDGES, 0)
    at = jnp.where(col < TILE[1], inside, beyond)
    at = jnp.where(cell < WL * WW, at, -1)
    lane = lax.broadcasted_iota(jnp.int32, (TOKENS, 128), 1)
    for k in range(3):
        picks_ref[:, k * 128 : (k + 1) * 128] = jnp.where(at == lane + k * 128, 1.0, 0.0).astype(bf16)


def weight_grads(side, scaled_ref, ctx_ref, cot_ref, dpacked_ref, to_ref):
    for block in range(4):
        if side and block > 1:
            pair = ctx_ref[...], cot_ref[:, (block - 2) * 256 : (block - 1) * 256]
        else:
            first = side * 2 * D + block * 256
            pair = scaled_ref[...], dpacked_ref[:, first : first + 256]
        part = dot(*pair, TN).astype(bf16)
        for k in range(2):
            at = (2 * block + k) * D
            to_ref[at : at + D, :] = part[:, k * 128 : (k + 1) * 128]


def attend_kernel(
    where_am_i,
    lat_ref, cot_ref, halo_lat_ref, halo_lon_ref, halo_cor_ref, gain_ref, w_qkv_ref, w_out_ref, picks_ref,
    other_ref, latent_s, cot_s, ctx_s, dpacked_s, scaled_s,
    packed_s, dctx_s,
):
    last_lat, core = where_am_i()
    picks = picks_ref[...]

    def gather(own, at):
        stack = jnp.concatenate(
            [own[HALF:, :], halo_lat_ref[at], halo_lon_ref[at], halo_cor_ref[at], jnp.zeros((48, D), bf16)],
            axis=0,
        )
        return dot(picks, stack)

    latent = gather(lat_ref, 0)
    latent_s[...] = latent.astype(bf16)
    cot_s[...] = gather(cot_ref, 1).astype(bf16)
    normed, _ = norm(latent)
    scaled_s[...] = (normed * gain_ref[...]).astype(bf16)
    packed_s[...] = dot(scaled_s[...], w_qkv_ref[...]).astype(bf16)
    dctx_s[...] = dot(cot_s[...], w_out_ref[...], NT).astype(bf16)

    scaling = HS ** (-0.5)
    key_at = lax.broadcasted_iota(jnp.int32, (ROWS, GROUP * ROWS), 0)
    lane = lax.broadcasted_iota(jnp.int32, (1, GROUP * ROWS), 1)
    query_at = lane
    for h in range(1, GROUP):
        query_at = query_at - jnp.where(lane >= h * ROWS, ROWS, 0)
    split = WL // 2 * WW
    differ = jnp.logical_and(last_lat, (key_at >= split) != (query_at >= split))
    excluded = jnp.logical_or(key_at >= WL * WW, differ)
    bias = jnp.where(excluded, -1e30, 0.0).astype(f32)
    head_of = lax.broadcasted_iota(jnp.int32, (GROUP, 1, SPAN), 2) // HS
    head = lax.broadcasted_iota(jnp.int32, (GROUP, 1, SPAN), 0)
    own_head = jnp.where(head_of == head, 1.0, 0.0).astype(f32)
    own_head_b = own_head.astype(bf16)

    def spread(rows):
        return (rows[None] * own_head_b).reshape(GROUP * ROWS, SPAN)

    def collect(rows):
        return jnp.sum(rows.reshape(GROUP, ROWS, SPAN) * own_head, axis=0).astype(bf16)

    for w in range(WINDOWS):
        for g in range(HEADS // GROUP):
            rows = slice(w * ROWS, (w + 1) * ROWS)
            at = [slice(b * D + g * SPAN, b * D + (g + 1) * SPAN) for b in range(3)]
            keys = packed_s[rows, at[1]]
            values = packed_s[rows, at[2]]
            queries = spread(packed_s[rows, at[0]])
            d_context = spread(dctx_s[rows, at[0]])
            scores = dot(keys, queries, NT) * (scaling * 1.4426950408889634) + bias
            expo = jnp.exp2(scores - jnp.max(scores, axis=0, keepdims=True))
            probs = expo * (1.0 / jnp.sum(expo, axis=0, keepdims=True))
            weights = probs.astype(bf16)
            d_weights = dot(values, d_context, NT)
            mean_d = jnp.sum(d_weights * probs, axis=0, keepdims=True)
            d_scaled = ((probs * scaling) * (d_weights - mean_d)).astype(bf16)
            ctx_s[rows, at[0]] = collect(dot(weights, values, TN))
            dpacked_s[rows, at[2]] = dot(weights, d_context).astype(bf16)
            dpacked_s[rows, at[0]] = collect(dot(d_scaled, keys, TN))
            dpacked_s[rows, at[1]] = dot(d_scaled, queries).astype(bf16)

    pl.when(core == 1)(lambda: weight_grads(0, scaled_s, ctx_s, cot_s, dpacked_s, other_ref))
    pl.when(core == 0)(lambda: weight_grads(1, scaled_s, ctx_s, cot_s, dpacked_s, other_ref))


def finish_kernel(
    where_am_i,
    latent_ref, cot_ref, ctx_ref, dpacked_ref, scaled_ref, gain_ref, w_qkv_ref, w_out_ref, picks_ref,
    own_ref, back_ref, back_lon_ref, gain_rows_ref, mine_ref,
):
    core = where_am_i()[1]
    pl.when(core == 0)(lambda: weight_grads(0, scaled_ref, ctx_ref, cot_ref, dpacked_ref, mine_ref))
    pl.when(core == 1)(lambda: weight_grads(1, scaled_ref, ctx_ref, cot_ref, dpacked_ref, mine_ref))
    latent = latent_ref[...].astype(f32)
    normed, recip_std = norm(latent)
    d_shifted = dot(dpacked_ref[...], w_qkv_ref[...], NT).astype(bf16).astype(f32)
    grad_gain = jnp.sum(d_shifted * normed, axis=0, keepdims=True)
    gain_rows_ref[...] = jnp.concatenate(
        [grad_gain[:, k * 128 : (k + 1) * 128] for k in range(4)] + [jnp.zeros((4, 128), f32)], axis=0
    ).astype(bf16)
    hidden = d_shifted * gain_ref[...]
    part = recip_std * (
        hidden
        - jnp.mean(hidden, axis=-1, keepdims=True)
        - normed * jnp.mean(hidden * normed, axis=-1, keepdims=True)
    )
    d_latent = (cot_ref[...].astype(f32) + part).astype(bf16)
    attn = dot(ctx_ref[...], w_out_ref[...]).astype(bf16).astype(f32)
    mixed = (latent + attn).astype(bf16)
    picks = picks_ref[...]
    for k, value in enumerate((mixed, d_latent)):
        moved = dot(picks, value, TN).astype(bf16)
        own_ref[k] = moved[:HALF]
        back_ref[k, :HALF] = moved[HALF : 2 * HALF]
        back_ref[k, HALF:] = moved[2 * HALF + EDGES : 2 * HALF + 2 * EDGES]
        back_lon_ref[k] = moved[2 * HALF : 2 * HALF + EDGES]


def here():
    return jnp.logical_and(lax.axis_index("x") == 3, lax.axis_index("yh") == 1), lax.axis_index("c")


def vmem_call(kernel, out_shapes, scratch, flops, moved, count, mebibytes=12):
    whole = pl.BlockSpec(memory_space=pltpu.VMEM)
    return pl.pallas_call(
        kernel,
        out_shape=out_shapes,
        in_specs=[whole] * count,
        out_specs=[whole] * len(out_shapes),
        scratch_shapes=scratch,
        compiler_params=pltpu.CompilerParams(vmem_limit_bytes=mebibytes * 1024 * 1024),
        cost_estimate=pl.CostEstimate(flops=flops, bytes_accessed=moved, transcendentals=0),
    )


def shape(*dims, dtype=bf16):
    return jax.ShapeDtypeStruct(dims, dtype)


def block(where_am_i, latent, cot, halo_lat, halo_lon, halo_cor, gain, w_qkv, w_out):
    picks, w_qkv, w_out = vmem_call(
        prepare_kernel, [shape(TOKENS, 384), shape(D, 3 * D), shape(D, D)], [], 1_000_000, 4_000_000, 2
    )(w_qkv, w_out)
    other, *kept = vmem_call(
        functools.partial(attend_kernel, where_am_i),
        [
            shape(STRIP, 128),
            shape(TOKENS, D), shape(TOKENS, D), shape(TOKENS, D), shape(TOKENS, 3 * D), shape(TOKENS, D),
        ],
        [pltpu.VMEM((TOKENS, 3 * D), bf16), pltpu.VMEM((TOKENS, D), bf16)],
        5_000_000_000, 8_000_000, 9, 32,
    )(latent, cot, halo_lat, halo_lon, halo_cor, gain, w_qkv, w_out, picks)
    own, back, back_lon, gain_rows, mine = vmem_call(
        functools.partial(finish_kernel, where_am_i),
        [shape(2, HALF, D), shape(2, BACK, D), shape(2, EDGES, D), shape(8, 128), shape(STRIP, 128)],
        [], 1_500_000_000, 4_000_000, 9, 32,
    )(*kept, gain, w_qkv, w_out, picks)
    return own, back, back_lon, mine, other, gain_rows


def add_kernel(mine_ref, arrived_ref, gain_ref, chunks_ref):
    for k in range(16):
        at = slice(k * CHUNK, (k + 1) * CHUNK)
        chunks_ref[k, :CHUNK] = (mine_ref[at, :].astype(f32) + arrived_ref[at, :].astype(f32)).astype(bf16)
        chunks_ref[k, CHUNK:] = gain_ref[...]


def spread_kernel(total_ref, arrived_ref, came_ref, back_lon_ref, spread_ref, edge_ref):
    total = (total_ref[...].astype(f32) + arrived_ref[...].astype(f32)).astype(bf16)
    for k in range(16):
        spread_ref[k] = total
    for k in range(2):
        edge_ref[k, :EDGES] = back_lon_ref[k]
        edge_ref[k, EDGES:] = came_ref[k, HALF:]


def unpack_kernel(where_am_i, side, half_ref, *refs):
    qkv_ref, out_ref = refs[3:5] if side else refs[:2]
    wide_s, sems = refs[-2:]
    core = where_am_i()[1]
    low = core == side

    def store(start):
        for block in range(4):
            cols = slice(block * 256, (block + 1) * 256)
            if start:
                for k in range(4 * block, 4 * block + 4):
                    at = slice(k // 2 * 128, (k // 2 + 1) * 128)
                    wide_s[k % 2 * CHUNK : (k % 2 + 1) * CHUNK, at] = half_ref[k, :CHUNK].astype(f32)

            def copy(ref, first):
                to = ref.at[:, first : first + 256]
                move = pltpu.make_async_copy(wide_s.at[:, cols], to, sems.at[block])
                move.start() if start else move.wait()

            pl.when(low)(lambda: copy(qkv_ref, block * 256))
            if block < 2:
                pl.when(jnp.logical_not(low))(lambda: copy(qkv_ref, 2 * D + block * 256))
            else:
                pl.when(jnp.logical_not(low))(lambda: copy(out_ref, block * 256 - D))

    if side:
        own_ref, gain_ref, gain_s, gain_sem = refs[0], refs[5], *refs[6:8]
        gain = half_ref[0, CHUNK:].astype(f32) + own_ref[0, CHUNK:].astype(f32)
        for k in range(4):
            gain_s[:, k * 128 : (k + 1) * 128] = gain[k : k + 1, :]
        move = pltpu.make_async_copy(gain_s, gain_ref, gain_sem)
        move.start()
    store(True)
    store(False)
    if side:
        move.wait()


def unpack(where_am_i, side, half, *rest):
    whole = pl.BlockSpec(memory_space=pltpu.VMEM)
    stay = pl.BlockSpec(memory_space=pltpu.HBM)
    outs = [shape(D, 3 * D, dtype=f32), shape(D, D, dtype=f32)]
    return pl.pallas_call(
        functools.partial(unpack_kernel, where_am_i, side),
        out_shape=outs + [shape(1, D, dtype=f32)] * side,
        in_specs=[whole] + [whole, stay, stay] * side,
        out_specs=[stay] * (2 + side),
        scratch_shapes=[pltpu.VMEM((1, D), f32), pltpu.SemaphoreType.DMA] * side
        + [pltpu.VMEM((D, 2 * D), f32), pltpu.SemaphoreType.DMA((4,))],
        input_output_aliases={2: 0, 3: 1} if side else {},
        compiler_params=pltpu.CompilerParams(vmem_limit_bytes=12 * 1024 * 1024),
        cost_estimate=pl.CostEstimate(flops=1_000_000, bytes_accessed=3_000_000, transcendentals=0),
    )(half, *rest)


def place_kernel(own_ref, came_ref, edge_ref, mixed_ref, d_latent_ref):
    for k, out_ref in enumerate((mixed_ref, d_latent_ref)):
        for r in range(3):
            at = r * TILE[1]
            for first, body_ref, edges in ((0, came_ref, EDGES), (HALF, own_ref, 0)):
                edge = edge_ref[k, edges + r * EDGE : edges + (r + 1) * EDGE].astype(f32)
                body = body_ref[k, at : at + EDGE].astype(f32)
                out_ref[first + at : first + at + EDGE, :] = (body + edge).astype(bf16)
                out_ref[first + at + EDGE : first + at + TILE[1], :] = body_ref[k, at + EDGE : at + TILE[1]]


def shifted(lat_by, lon_by):
    pairs = []
    for i in range(256):
        lat, lon = i // 32, i % 32
        pairs.append((i, (lat + lat_by) % 8 * 32 + (lon + lon_by) % 32))
    return pairs


def swapped(bits):
    return [(i, i ^ bits) for i in range(256)]


def send(value, pairs):
    return lax.ppermute(value, ALL, pairs)


def sum_and_return(own, back, back_lon, mine, other, gain_rows):
    arrived = send(other, swapped(1))
    chunks = vmem_call(
        add_kernel, [shape(16, SUMMED, 128)], [], 1_000_000, 4_000_000, 3
    )(mine, arrived, gain_rows)[0]
    pieces = lax.all_to_all(chunks, PLANE, 0, 0, tiled=True)
    total = jnp.sum(pieces.astype(f32), axis=0).astype(bf16)
    for bits in (2, 4):
        total = (total.astype(f32) + send(total, swapped(bits)).astype(f32)).astype(bf16)
    came = send(back, shifted(1, 0))
    spread, edge = vmem_call(
        spread_kernel, [shape(16, SUMMED, 128), shape(2, 2 * EDGES, D)], [], 1_000_000, 3_000_000, 4
    )(total, send(total, swapped(12)), came, back_lon)
    half = lax.all_to_all(spread, PLANE, 0, 0, tiled=True)
    edge = send(edge, shifted(0, 1))
    half, edge = lax.optimization_barrier((half, edge))
    arrived = send(half, swapped(1))
    parts = unpack(here, 0, half)
    mixed, d_latent = vmem_call(
        place_kernel, [shape(2 * HALF, D), shape(2 * HALF, D)], [], 1_000_000, 2_000_000, 3
    )(own, came, edge)
    grad_qkv, grad_out, grad_gain = unpack(here, 1, arrived, half, *parts)
    return mixed.reshape(*TILE, D), d_latent.reshape(*TILE, D), grad_qkv, grad_out, grad_gain.reshape(D)


def local(latent, norm_gain, w_qkv, w_out, cotangent):
    both = jnp.stack([latent[:3], cotangent[:3]])
    halo_lat = send(both.reshape(2, HALF, D), shifted(-1, 0))
    halo_cor = send(both[:, :, :EDGE].reshape(2, EDGES, D), shifted(-1, -1))
    edge = jnp.stack([latent[3:, :EDGE], cotangent[3:, :EDGE]])
    halo_lon = send(edge.reshape(2, EDGES, D), shifted(0, -1))
    return sum_and_return(*block(
        here, latent.reshape(-1, D), cotangent.reshape(-1, D), halo_lat, halo_lon, halo_cor,
        norm_gain.reshape(1, D), w_qkv, w_out,
    ))


def solution(mesh):
    fine = Mesh(mesh.devices.reshape(4, 2, 2, 8, 2), ALL)
    in_specs = (P(LAT, LON, None), P(), P(), P(), P(LAT, LON, None))
    out_specs = (P(LAT, LON, None), P(LAT, LON, None), P(), P(), P())
    return jax.shard_map(local, mesh=fine, in_specs=in_specs, out_specs=out_specs, check_vma=False)
```

```python
import functools

import jax
import jax.numpy as jnp
from jax import lax
from jax.experimental import pallas as pl
from jax.experimental.pallas import tpu as pltpu
from jax.sharding import Mesh, PartitionSpec as P

ALL = ("xh", "xl", "yh", "yl", "zh", "zm", "zl", "c")
LAT = ALL[:3]
LON = ALL[3:]
BOX = ("xl", "yh", "yl", "zl")
HEADS = 16
HS = 32
WL = 6
WW = 12
TILE = (6, 48)
D = 512
WINDOWS = 4
ROWS = 80
TOKENS = WINDOWS * ROWS
GROUP = 8
SPAN = GROUP * HS
EDGE = 8
HALF = 3 * TILE[1]
EDGES = 3 * EDGE
STRIP = 512 * 8
CHUNK = STRIP // 16
SUMMED = CHUNK + 8
BACK = HALF + EDGES
f32 = jnp.float32
bf16 = jnp.bfloat16
NT = (((1,), (1,)), ((), ()))
TN = (((0,), (0,)), ((), ()))


def dot(a, b, dims=(((1,), (0,)), ((), ()))):
    return lax.dot_general(a, b, dims, preferred_element_type=f32)


def norm(latent):
    centred = latent - jnp.mean(latent, axis=-1, keepdims=True)
    variance = jnp.mean(centred * centred, axis=-1, keepdims=True)
    recip_std = lax.rsqrt(variance + 1e-05)
    return centred * recip_std, recip_std


def edges_kernel(rows_ref, edge_ref, to_cor_ref, to_lon_ref):
    for k in range(2):
        for r in range(3):
            at = slice(r * EDGE, (r + 1) * EDGE)
            to_cor_ref[k, at] = rows_ref[k, r, :EDGE]
            to_lon_ref[k, at] = edge_ref[k, r, :EDGE]


def prepare_kernel(w_qkv_ref, w_out_ref, picks_ref, w_qkv_s, w_out_s):
    w_qkv_s[...] = w_qkv_ref[...]
    w_out_s[...] = w_out_ref[...]
    def count(value, step, upto):
        return sum(jnp.where(value >= step * k, 1, 0) for k in range(1, upto))

    row = lax.broadcasted_iota(jnp.int32, (TOKENS, 128), 0)
    window = count(row, ROWS, WINDOWS)
    cell = row - window * ROWS
    line = count(cell, WW, WL)
    col = (window + 0) * WW + cell - line * WW + WW // 2
    below = line >= WL // 2
    line = jnp.where(below, line - WL // 2, line)
    inside = line * TILE[1] + col + jnp.where(below, HALF, 0)
    beyond = 2 * HALF + line * EDGE + col - TILE[1] + jnp.where(below, EDGES, 0)
    at = jnp.where(col < TILE[1], inside, beyond)
    at = jnp.where(cell < WL * WW, at, -1)
    lane = lax.broadcasted_iota(jnp.int32, (TOKENS, 128), 1)
    for k in range(3):
        picks_ref[:, k * 128 : (k + 1) * 128] = jnp.where(at == lane + k * 128, 1.0, 0.0).astype(bf16)


def weight_grads(side, scaled_ref, ctx_ref, cot_ref, dpacked_ref, to_ref):
    for block in range(4):
        if side and block > 1:
            pair = ctx_ref[...], cot_ref[:, (block - 2) * 256 : (block - 1) * 256]
        else:
            first = side * 2 * D + block * 256
            pair = scaled_ref[...], dpacked_ref[:, first : first + 256]
        part = dot(*pair, TN).astype(bf16)
        for k in range(2):
            at = (2 * block + k) * D
            to_ref[at : at + D, :] = part[:, k * 128 : (k + 1) * 128]


def attend_kernel(
    where_am_i,
    lat_ref, cot_ref, halo_lat_ref, halo_lon_ref, halo_cor_ref, gain_ref, w_qkv_ref, w_out_ref, picks_ref,
    other_ref, latent_s, cot_s, ctx_s, dpacked_s, scaled_s,
    packed_s, dctx_s,
):
    last_lat, core = where_am_i()
    picks = picks_ref[...]

    def gather(own, at):
        stack = jnp.concatenate(
            [own[HALF:, :], halo_lat_ref[at], halo_lon_ref[at], halo_cor_ref[at], jnp.zeros((48, D), bf16)],
            axis=0,
        )
        return dot(picks, stack)

    latent = gather(lat_ref, 0)
    latent_s[...] = latent.astype(bf16)
    cot_s[...] = gather(cot_ref, 1).astype(bf16)
    normed, _ = norm(latent)
    scaled_s[...] = (normed * gain_ref[...]).astype(bf16)
    packed_s[...] = dot(scaled_s[...], w_qkv_ref[...]).astype(bf16)
    dctx_s[...] = dot(cot_s[...], w_out_ref[...], NT).astype(bf16)

    scaling = HS ** (-0.5)
    key_at = lax.broadcasted_iota(jnp.int32, (ROWS, GROUP * ROWS), 0)
    lane = lax.broadcasted_iota(jnp.int32, (1, GROUP * ROWS), 1)
    query_at = lane
    for h in range(1, GROUP):
        query_at = query_at - jnp.where(lane >= h * ROWS, ROWS, 0)
    split = WL // 2 * WW
    differ = jnp.logical_and(last_lat, (key_at >= split) != (query_at >= split))
    excluded = jnp.logical_or(key_at >= WL * WW, differ)
    bias = jnp.where(excluded, -1e30, 0.0).astype(f32)
    head_of = lax.broadcasted_iota(jnp.int32, (GROUP, 1, SPAN), 2) // HS
    head = lax.broadcasted_iota(jnp.int32, (GROUP, 1, SPAN), 0)
    own_head = jnp.where(head_of == head, 1.0, 0.0).astype(f32)
    own_head_b = own_head.astype(bf16)

    def spread(rows):
        return (rows[None] * own_head_b).reshape(GROUP * ROWS, SPAN)

    def collect(rows):
        return jnp.sum(rows.reshape(GROUP, ROWS, SPAN) * own_head, axis=0).astype(bf16)

    def begin(w, g):
        rows = slice(w * ROWS, (w + 1) * ROWS)
        at = [slice(b * D + g * SPAN, b * D + (g + 1) * SPAN) for b in range(3)]
        keys = packed_s[rows, at[1]]
        values = packed_s[rows, at[2]]
        queries = spread(packed_s[rows, at[0]])
        d_context = spread(dctx_s[rows, at[0]])
        return rows, at, keys, values, queries, d_context, dot(keys, queries, NT), dot(values, d_context, NT)

    def end(rows, at, keys, values, queries, d_context, scores, d_weights):
        scores = scores * (scaling * 1.4426950408889634) + bias
        expo = jnp.exp2(scores - jnp.max(scores, axis=0, keepdims=True))
        probs = expo * (1.0 / jnp.sum(expo, axis=0, keepdims=True))
        weights = probs.astype(bf16)
        mean_d = jnp.sum(d_weights * probs, axis=0, keepdims=True)
        d_scaled = ((probs * scaling) * (d_weights - mean_d)).astype(bf16)
        ctx_s[rows, at[0]] = collect(dot(weights, values, TN))
        dpacked_s[rows, at[2]] = dot(weights, d_context).astype(bf16)
        dpacked_s[rows, at[0]] = collect(dot(d_scaled, keys, TN))
        dpacked_s[rows, at[1]] = dot(d_scaled, queries).astype(bf16)

    todo = [(w, g) for w in range(WINDOWS) for g in range(HEADS // GROUP)]
    begun = begin(*todo[0])
    for k in range(1, len(todo) + 1):
        later = begin(*todo[k]) if k < len(todo) else None
        end(*begun)
        begun = later

    pl.when(core == 1)(lambda: weight_grads(0, scaled_s, ctx_s, cot_s, dpacked_s, other_ref))
    pl.when(core == 0)(lambda: weight_grads(1, scaled_s, ctx_s, cot_s, dpacked_s, other_ref))


def finish_kernel(
    where_am_i,
    latent_ref, cot_ref, ctx_ref, dpacked_ref, scaled_ref, gain_ref, w_qkv_ref, w_out_ref, picks_ref,
    own_ref, back_ref, back_lon_ref, gain_rows_ref, mine_ref,
):
    core = where_am_i()[1]
    pl.when(core == 0)(lambda: weight_grads(0, scaled_ref, ctx_ref, cot_ref, dpacked_ref, mine_ref))
    pl.when(core == 1)(lambda: weight_grads(1, scaled_ref, ctx_ref, cot_ref, dpacked_ref, mine_ref))
    latent = latent_ref[...].astype(f32)
    normed, recip_std = norm(latent)
    d_shifted = dot(dpacked_ref[...], w_qkv_ref[...], NT).astype(bf16).astype(f32)
    grad_gain = jnp.sum(d_shifted * normed, axis=0, keepdims=True)
    gain_rows_ref[...] = jnp.concatenate(
        [grad_gain[:, k * 128 : (k + 1) * 128] for k in range(4)] + [jnp.zeros((4, 128), f32)], axis=0
    ).astype(bf16)
    hidden = d_shifted * gain_ref[...]
    part = recip_std * (
        hidden
        - jnp.mean(hidden, axis=-1, keepdims=True)
        - normed * jnp.mean(hidden * normed, axis=-1, keepdims=True)
    )
    d_latent = (cot_ref[...].astype(f32) + part).astype(bf16)
    attn = dot(ctx_ref[...], w_out_ref[...]).astype(bf16).astype(f32)
    mixed = (latent + attn).astype(bf16)
    picks = picks_ref[...]
    for k, value in enumerate((mixed, d_latent)):
        moved = dot(picks, value, TN).astype(bf16)
        own_ref[k] = moved[:HALF]
        back_ref[k, :HALF] = moved[HALF : 2 * HALF]
        back_ref[k, HALF:] = moved[2 * HALF + EDGES : 2 * HALF + 2 * EDGES]
        back_lon_ref[k] = moved[2 * HALF : 2 * HALF + EDGES]


def here():
    last_lat = lax.axis_index("xh") + lax.axis_index("xl") + lax.axis_index("yh") == 3
    return last_lat, lax.axis_index("c")


def moved_chunk(k):
    return lax.rem(k + 8 * lax.axis_index("xh"), 16)


def vmem_call(kernel, out_shapes, scratch, flops, moved, count, mebibytes=12):
    whole = pl.BlockSpec(memory_space=pltpu.VMEM)
    return pl.pallas_call(
        kernel,
        out_shape=out_shapes,
        in_specs=[whole] * count,
        out_specs=[whole] * len(out_shapes),
        scratch_shapes=scratch,
        compiler_params=pltpu.CompilerParams(vmem_limit_bytes=mebibytes * 1024 * 1024),
        cost_estimate=pl.CostEstimate(flops=flops, bytes_accessed=moved, transcendentals=0),
    )


def shape(*dims, dtype=bf16):
    return jax.ShapeDtypeStruct(dims, dtype)


def block(where_am_i, latent, cot, halo_lat, halo_lon, halo_cor, gain, w_qkv, w_out):
    picks, w_qkv, w_out = vmem_call(
        prepare_kernel, [shape(TOKENS, 384), shape(D, 3 * D), shape(D, D)], [], 1_000_000, 4_000_000, 2
    )(w_qkv, w_out)
    other, *kept = vmem_call(
        functools.partial(attend_kernel, where_am_i),
        [
            shape(STRIP, 128),
            shape(TOKENS, D), shape(TOKENS, D), shape(TOKENS, D), shape(TOKENS, 3 * D), shape(TOKENS, D),
        ],
        [pltpu.VMEM((TOKENS, 3 * D), bf16), pltpu.VMEM((TOKENS, D), bf16)],
        5_000_000_000, 8_000_000, 9, 32,
    )(latent, cot, halo_lat, halo_lon, halo_cor, gain, w_qkv, w_out, picks)
    own, back, back_lon, gain_rows, mine = vmem_call(
        functools.partial(finish_kernel, where_am_i),
        [shape(2, HALF, D), shape(2, BACK, D), shape(2, EDGES, D), shape(8, 128), shape(STRIP, 128)],
        [], 1_500_000_000, 4_000_000, 9, 32,
    )(*kept, gain, w_qkv, w_out, picks)
    return own, back, back_lon, mine, other, gain_rows


def add_kernel(mine_ref, arrived_ref, gain_ref, chunks_ref):
    for k in range(16):
        at = slice(k * CHUNK, (k + 1) * CHUNK)
        to = moved_chunk(k)
        chunks_ref[to, :CHUNK] = (mine_ref[at, :].astype(f32) + arrived_ref[at, :].astype(f32)).astype(bf16)
        chunks_ref[to, CHUNK:] = gain_ref[...]


def edge_kernel(came_ref, back_lon_ref, edge_ref):
    for k in range(2):
        edge_ref[k, :EDGES] = back_lon_ref[k]
        edge_ref[k, EDGES:] = came_ref[k, HALF:]


def unpack_kernel(where_am_i, side, half_ref, *refs):
    qkv_ref, out_ref = refs[3:5] if side else refs[:2]
    wide_s, sems = refs[-2:]
    core = where_am_i()[1]
    low = core == side

    def store(start):
        for block in range(4):
            cols = slice(block * 256, (block + 1) * 256)
            if start:
                for k in range(4 * block, 4 * block + 4):
                    at = slice(k // 2 * 128, (k // 2 + 1) * 128)
                    wide_s[k % 2 * CHUNK : (k % 2 + 1) * CHUNK, at] = half_ref[moved_chunk(k), :CHUNK].astype(f32)

            def copy(ref, first):
                to = ref.at[:, first : first + 256]
                move = pltpu.make_async_copy(wide_s.at[:, cols], to, sems.at[block])
                move.start() if start else move.wait()

            pl.when(low)(lambda: copy(qkv_ref, block * 256))
            if block < 2:
                pl.when(jnp.logical_not(low))(lambda: copy(qkv_ref, 2 * D + block * 256))
            else:
                pl.when(jnp.logical_not(low))(lambda: copy(out_ref, block * 256 - D))

    if side:
        own_ref, gain_ref, gain_s, gain_sem = refs[0], refs[5], *refs[6:8]
        at = moved_chunk(0)
        gain = half_ref[at, CHUNK:].astype(f32) + own_ref[at, CHUNK:].astype(f32)
        for k in range(4):
            gain_s[:, k * 128 : (k + 1) * 128] = gain[k : k + 1, :]
        move = pltpu.make_async_copy(gain_s, gain_ref, gain_sem)
        move.start()
    store(True)
    store(False)
    if side:
        move.wait()


def unpack(where_am_i, side, half, *rest):
    whole = pl.BlockSpec(memory_space=pltpu.VMEM)
    stay = pl.BlockSpec(memory_space=pltpu.HBM)
    outs = [shape(D, 3 * D, dtype=f32), shape(D, D, dtype=f32)]
    return pl.pallas_call(
        functools.partial(unpack_kernel, where_am_i, side),
        out_shape=outs + [shape(1, D, dtype=f32)] * side,
        in_specs=[whole] + [whole, stay, stay] * side,
        out_specs=[stay] * (2 + side),
        scratch_shapes=[pltpu.VMEM((1, D), f32), pltpu.SemaphoreType.DMA] * side
        + [pltpu.VMEM((D, 2 * D), f32), pltpu.SemaphoreType.DMA((4,))],
        input_output_aliases={2: 0, 3: 1} if side else {},
        compiler_params=pltpu.CompilerParams(vmem_limit_bytes=12 * 1024 * 1024),
        cost_estimate=pl.CostEstimate(flops=1_000_000, bytes_accessed=3_000_000, transcendentals=0),
    )(half, *rest)


def place_kernel(own_ref, came_ref, edge_ref, mixed_ref, d_latent_ref):
    for k, out_ref in enumerate((mixed_ref, d_latent_ref)):
        for r in range(3):
            at = r * TILE[1]
            for first, body_ref, edges in ((0, came_ref, EDGES), (HALF, own_ref, 0)):
                edge = edge_ref[k, edges + r * EDGE : edges + (r + 1) * EDGE].astype(f32)
                body = body_ref[k, at : at + EDGE].astype(f32)
                out_ref[first + at : first + at + EDGE, :] = (body + edge).astype(bf16)
                out_ref[first + at + EDGE : first + at + TILE[1], :] = body_ref[k, at + EDGE : at + TILE[1]]


def shifted(lat_by, lon_by):
    pairs = []
    for i in range(256):
        lat, lon = i // 32, i % 32
        pairs.append((i, (lat + lat_by) % 8 * 32 + (lon + lon_by) % 32))
    return pairs


def swapped(bits):
    return [(i, i ^ bits) for i in range(256)]


def send(value, pairs):
    return lax.ppermute(value, ALL, pairs)


def sum_and_return(own, back, back_lon, mine, other, gain_rows):
    arrived = send(other, swapped(1))
    chunks = vmem_call(
        add_kernel, [shape(16, SUMMED, 128)], [], 1_000_000, 4_000_000, 3
    )(mine, arrived, gain_rows)[0]
    pieces = lax.all_to_all(chunks, BOX, 0, 0, tiled=True)
    total = jnp.sum(pieces.astype(f32), axis=0).astype(bf16)
    for bits in (192, 4, 12):
        total = (total.astype(f32) + send(total, swapped(bits)).astype(f32)).astype(bf16)
    came = send(back, shifted(1, 0))
    edge = vmem_call(edge_kernel, [shape(2, 2 * EDGES, D)], [], 1_000_000, 1_000_000, 2)(came, back_lon)[0]
    total, edge = lax.optimization_barrier((total, edge))
    half = lax.all_to_all(jnp.broadcast_to(total, (16, SUMMED, 128)), BOX, 0, 0, tiled=True)
    edge = send(edge, shifted(0, 1))
    mixed, d_latent = vmem_call(
        place_kernel, [shape(2 * HALF, D), shape(2 * HALF, D)], [], 1_000_000, 2_000_000, 3
    )(own, came, edge)
    half, mixed, d_latent = lax.optimization_barrier((half, mixed, d_latent))
    arrived = send(half, swapped(1))
    parts = unpack(here, 0, half)
    grad_qkv, grad_out, grad_gain = unpack(here, 1, arrived, half, *parts)
    return mixed.reshape(*TILE, D), d_latent.reshape(*TILE, D), grad_qkv, grad_out, grad_gain.reshape(D)


def local(latent, norm_gain, w_qkv, w_out, cotangent):
    both = jnp.stack([latent[:3], cotangent[:3]])
    halo_lat = send(both.reshape(2, HALF, D), shifted(-1, 0))
    edge = jnp.stack([latent[3:, :16], cotangent[3:, :16]])
    to_cor, to_lon = vmem_call(
        edges_kernel, [shape(2, EDGES, D), shape(2, EDGES, D)], [], 1_000_000, 500_000, 2
    )(both, edge)
    halo_cor = send(to_cor, shifted(-1, -1))
    halo_lon = send(to_lon, shifted(0, -1))
    return sum_and_return(*block(
        here, latent.reshape(-1, D), cotangent.reshape(-1, D), halo_lat, halo_lon, halo_cor,
        norm_gain.reshape(1, D), w_qkv, w_out,
    ))


def solution(mesh):
    fine = Mesh(mesh.devices.reshape((2,) * 8), ALL)
    in_specs = (P(LAT, LON, None), P(), P(), P(), P(LAT, LON, None))
    out_specs = (P(LAT, LON, None), P(LAT, LON, None), P(), P(), P())
    return jax.shard_map(local, mesh=fine, in_specs=in_specs, out_specs=out_specs, check_vma=False)
```

```python
import functools

import jax
import jax.numpy as jnp
from jax import lax
from jax.experimental import pallas as pl
from jax.experimental.pallas import tpu as pltpu
from jax.sharding import Mesh, PartitionSpec as P

ALL = ("xh", "xl", "yh", "yl", "zh", "zm", "zl", "c")
LAT = ALL[:3]
LON = ALL[3:]
BOX = ("xl", "yh", "yl", "zl")
HEADS = 16
HS = 32
WL = 6
WW = 12
TILE = (6, 48)
D = 512
WINDOWS = 4
ROWS = 80
TOKENS = WINDOWS * ROWS
GROUP = 8
SPAN = GROUP * HS
EDGE = 8
HALF = 3 * TILE[1]
EDGES = 3 * EDGE
STRIP = 512 * 8
CHUNK = STRIP // 16
SUMMED = CHUNK + 8
BACK = HALF + EDGES
f32 = jnp.float32
bf16 = jnp.bfloat16
NT = (((1,), (1,)), ((), ()))
TN = (((0,), (0,)), ((), ()))


def dot(a, b, dims=(((1,), (0,)), ((), ()))):
    return lax.dot_general(a, b, dims, preferred_element_type=f32)


def norm(latent):
    centred = latent - jnp.mean(latent, axis=-1, keepdims=True)
    variance = jnp.mean(centred * centred, axis=-1, keepdims=True)
    recip_std = lax.rsqrt(variance + 1e-05)
    return centred * recip_std, recip_std


def edges_kernel(rows_ref, edge_ref, to_cor_ref, to_lon_ref):
    for k in range(2):
        for r in range(3):
            at = slice(r * EDGE, (r + 1) * EDGE)
            to_cor_ref[k, at] = rows_ref[k, r, :EDGE]
            to_lon_ref[k, at] = edge_ref[k, r, :EDGE]


def prepare_kernel(w_qkv_ref, w_out_ref, picks_ref, w_qkv_s, w_out_s):
    w_qkv_s[...] = w_qkv_ref[...]
    w_out_s[...] = w_out_ref[...]
    def count(value, step, upto):
        return sum(jnp.where(value >= step * k, 1, 0) for k in range(1, upto))

    row = lax.broadcasted_iota(jnp.int32, (TOKENS, 128), 0)
    window = count(row, ROWS, WINDOWS)
    cell = row - window * ROWS
    line = count(cell, WW, WL)
    col = (window + 0) * WW + cell - line * WW + WW // 2
    below = line >= WL // 2
    line = jnp.where(below, line - WL // 2, line)
    inside = line * TILE[1] + col + jnp.where(below, HALF, 0)
    beyond = 2 * HALF + line * EDGE + col - TILE[1] + jnp.where(below, EDGES, 0)
    at = jnp.where(col < TILE[1], inside, beyond)
    at = jnp.where(cell < WL * WW, at, -1)
    lane = lax.broadcasted_iota(jnp.int32, (TOKENS, 128), 1)
    for k in range(3):
        picks_ref[:, k * 128 : (k + 1) * 128] = jnp.where(at == lane + k * 128, 1.0, 0.0).astype(bf16)


def weight_grads(side, scaled_ref, ctx_ref, cot_ref, dpacked_ref, to_ref):
    for block in range(4):
        if side and block > 1:
            pair = ctx_ref[...], cot_ref[:, (block - 2) * 256 : (block - 1) * 256]
        else:
            first = side * 2 * D + block * 256
            pair = scaled_ref[...], dpacked_ref[:, first : first + 256]
        part = dot(*pair, TN).astype(bf16)
        for k in range(2):
            at = (2 * block + k) * D
            to_ref[at : at + D, :] = part[:, k * 128 : (k + 1) * 128]


def attend_kernel(
    where_am_i,
    lat_ref, cot_ref, halo_lat_ref, halo_lon_ref, halo_cor_ref, gain_ref, w_qkv_ref, w_out_ref, picks_ref,
    other_ref, latent_s, cot_s, ctx_s, dpacked_s, scaled_s,
    packed_s, dctx_s,
):
    last_lat, core = where_am_i()
    picks = picks_ref[...]

    def gather(own, at):
        stack = jnp.concatenate(
            [own[HALF:, :], halo_lat_ref[at], halo_lon_ref[at], halo_cor_ref[at], jnp.zeros((48, D), bf16)],
            axis=0,
        )
        return dot(picks, stack)

    latent = gather(lat_ref, 0)
    latent_s[...] = latent.astype(bf16)
    cot_s[...] = gather(cot_ref, 1).astype(bf16)
    normed, _ = norm(latent)
    scaled_s[...] = (normed * gain_ref[...]).astype(bf16)
    packed_s[...] = dot(scaled_s[...], w_qkv_ref[...]).astype(bf16)
    dctx_s[...] = dot(cot_s[...], w_out_ref[...], NT).astype(bf16)

    scaling = HS ** (-0.5)
    key_at = lax.broadcasted_iota(jnp.int32, (ROWS, GROUP * ROWS), 0)
    lane = lax.broadcasted_iota(jnp.int32, (1, GROUP * ROWS), 1)
    query_at = lane
    for h in range(1, GROUP):
        query_at = query_at - jnp.where(lane >= h * ROWS, ROWS, 0)
    split = WL // 2 * WW
    differ = jnp.logical_and(last_lat, (key_at >= split) != (query_at >= split))
    excluded = jnp.logical_or(key_at >= WL * WW, differ)
    bias = jnp.where(excluded, -1e30, 0.0).astype(f32)
    head_of = lax.broadcasted_iota(jnp.int32, (GROUP, 1, SPAN), 2) // HS
    head = lax.broadcasted_iota(jnp.int32, (GROUP, 1, SPAN), 0)
    own_head = jnp.where(head_of == head, 1.0, 0.0).astype(f32)
    own_head_b = own_head.astype(bf16)

    def spread(rows):
        return (rows[None] * own_head_b).reshape(GROUP * ROWS, SPAN)

    def collect(rows):
        return jnp.sum(rows.reshape(GROUP, ROWS, SPAN) * own_head, axis=0).astype(bf16)

    def begin(w, g):
        rows = slice(w * ROWS, (w + 1) * ROWS)
        at = [slice(b * D + g * SPAN, b * D + (g + 1) * SPAN) for b in range(3)]
        keys = packed_s[rows, at[1]]
        values = packed_s[rows, at[2]]
        queries = spread(packed_s[rows, at[0]])
        d_context = spread(dctx_s[rows, at[0]])
        return rows, at, keys, values, queries, d_context, dot(keys, queries, NT), dot(values, d_context, NT)

    def end(rows, at, keys, values, queries, d_context, scores, d_weights):
        scores = scores * (scaling * 1.4426950408889634) + bias
        expo = jnp.exp2(scores - jnp.max(scores, axis=0, keepdims=True))
        probs = expo * (1.0 / jnp.sum(expo, axis=0, keepdims=True))
        weights = probs.astype(bf16)
        mean_d = jnp.sum(d_weights * probs, axis=0, keepdims=True)
        d_scaled = ((probs * scaling) * (d_weights - mean_d)).astype(bf16)
        ctx_s[rows, at[0]] = collect(dot(weights, values, TN))
        dpacked_s[rows, at[2]] = dot(weights, d_context).astype(bf16)
        dpacked_s[rows, at[0]] = collect(dot(d_scaled, keys, TN))
        dpacked_s[rows, at[1]] = dot(d_scaled, queries).astype(bf16)

    todo = [(w, g) for w in range(WINDOWS) for g in range(HEADS // GROUP)]
    begun = begin(*todo[0])
    for k in range(1, len(todo) + 1):
        later = begin(*todo[k]) if k < len(todo) else None
        end(*begun)
        begun = later

    pl.when(core == 1)(lambda: weight_grads(0, scaled_s, ctx_s, cot_s, dpacked_s, other_ref))
    pl.when(core == 0)(lambda: weight_grads(1, scaled_s, ctx_s, cot_s, dpacked_s, other_ref))


def finish(
    side,
    latent_ref, cot_ref, ctx_ref, dpacked_ref, scaled_ref, gain_ref, w_qkv_ref, w_out_ref, picks_ref,
    own_ref, back_ref, back_lon_ref, gain_rows_ref, mine_ref,
):
    weight_grads(side, scaled_ref, ctx_ref, cot_ref, dpacked_ref, mine_ref)
    latent = latent_ref[...].astype(f32)
    normed, recip_std = norm(latent)
    d_shifted = dot(dpacked_ref[...], w_qkv_ref[...], NT).astype(bf16).astype(f32)
    grad_gain = jnp.sum(d_shifted * normed, axis=0, keepdims=True)
    gain_rows_ref[...] = jnp.concatenate(
        [grad_gain[:, k * 128 : (k + 1) * 128] for k in range(4)] + [jnp.zeros((4, 128), f32)], axis=0
    ).astype(bf16)
    hidden = d_shifted * gain_ref[...]
    part = recip_std * (
        hidden
        - jnp.mean(hidden, axis=-1, keepdims=True)
        - normed * jnp.mean(hidden * normed, axis=-1, keepdims=True)
    )
    d_latent = (cot_ref[...].astype(f32) + part).astype(bf16)
    attn = dot(ctx_ref[...], w_out_ref[...]).astype(bf16).astype(f32)
    mixed = (latent + attn).astype(bf16)
    picks = picks_ref[...]
    for k, value in enumerate((mixed, d_latent)):
        moved = dot(picks, value, TN).astype(bf16)
        own_ref[k] = moved[:HALF]
        back_ref[k, :HALF] = moved[HALF : 2 * HALF]
        back_ref[k, HALF:] = moved[2 * HALF + EDGES : 2 * HALF + 2 * EDGES]
        back_lon_ref[k] = moved[2 * HALF : 2 * HALF + EDGES]


def finish_kernel(where_am_i, *refs):
    pl.when(where_am_i()[1] == 1)(lambda: finish(1, *refs))


def here():
    last_lat = lax.axis_index("xh") + lax.axis_index("xl") + lax.axis_index("yh") == 3
    return last_lat, lax.axis_index("c")


def moved_chunk(k):
    return lax.rem(k + 8 * lax.axis_index("xh"), 16)


def vmem_call(kernel, out_shapes, scratch, flops, moved, count, mebibytes=12):
    whole = pl.BlockSpec(memory_space=pltpu.VMEM)
    return pl.pallas_call(
        kernel,
        out_shape=out_shapes,
        in_specs=[whole] * count,
        out_specs=[whole] * len(out_shapes),
        scratch_shapes=scratch,
        compiler_params=pltpu.CompilerParams(vmem_limit_bytes=mebibytes * 1024 * 1024),
        cost_estimate=pl.CostEstimate(flops=flops, bytes_accessed=moved, transcendentals=0),
    )


def shape(*dims, dtype=bf16):
    return jax.ShapeDtypeStruct(dims, dtype)


FINISHED = [shape(2, HALF, D), shape(2, BACK, D), shape(2, EDGES, D), shape(8, 128), shape(STRIP, 128)]


def block(where_am_i, latent, cot, halo_lat, halo_lon, halo_cor, gain, w_qkv, w_out):
    picks, w_qkv, w_out = vmem_call(
        prepare_kernel, [shape(TOKENS, 384), shape(D, 3 * D), shape(D, D)], [], 1_000_000, 4_000_000, 2
    )(w_qkv, w_out)
    other, *kept = vmem_call(
        functools.partial(attend_kernel, where_am_i),
        [
            shape(STRIP, 128),
            shape(TOKENS, D), shape(TOKENS, D), shape(TOKENS, D), shape(TOKENS, 3 * D), shape(TOKENS, D),
        ],
        [pltpu.VMEM((TOKENS, 3 * D), bf16), pltpu.VMEM((TOKENS, D), bf16)],
        5_000_000_000, 8_000_000, 9, 32,
    )(latent, cot, halo_lat, halo_lon, halo_cor, gain, w_qkv, w_out, picks)
    operands = (*kept, gain, w_qkv, w_out, picks)
    finished = vmem_call(
        functools.partial(finish_kernel, where_am_i), FINISHED, [], 1_500_000_000, 4_000_000, 9, 24
    )(*operands)
    return other, operands, finished


def add_kernel(where_am_i, arrived_ref, *refs):
    operands, early, outs = refs[:9], refs[9:14], refs[14:17]
    chunks_ref, gain_s, mine_s = refs[17:]
    core = where_am_i()[1]

    def add_to_arrived(gain_ref, mine_ref):
        for k in range(16):
            at = slice(k * CHUNK, (k + 1) * CHUNK)
            to = moved_chunk(k)
            chunks_ref[to, :CHUNK] = (mine_ref[at, :].astype(f32) + arrived_ref[at, :].astype(f32)).astype(bf16)
            chunks_ref[to, CHUNK:] = gain_ref[...]

    @pl.when(core == 0)
    def _():
        finish(0, *operands, *outs, gain_s, mine_s)
        add_to_arrived(gain_s, mine_s)

    @pl.when(core == 1)
    def _():
        add_to_arrived(*early[3:])
        for out_ref, early_ref in zip(outs, early):
            out_ref[...] = early_ref[...]


def add(where_am_i, arrived, operands, finished):
    whole = pl.BlockSpec(memory_space=pltpu.VMEM)
    return pl.pallas_call(
        functools.partial(add_kernel, where_am_i),
        out_shape=FINISHED[:3] + [shape(16, SUMMED, 128)],
        in_specs=[whole] * 15,
        out_specs=[whole] * 4,
        scratch_shapes=[pltpu.VMEM((8, 128), bf16), pltpu.VMEM((STRIP, 128), bf16)],
        compiler_params=pltpu.CompilerParams(vmem_limit_bytes=24 * 1024 * 1024),
        cost_estimate=pl.CostEstimate(flops=1_500_000_000, bytes_accessed=4_000_000, transcendentals=0),
    )(arrived, *operands, *finished)


def edge_kernel(came_ref, back_lon_ref, edge_ref):
    for k in range(2):
        edge_ref[k, :EDGES] = back_lon_ref[k]
        edge_ref[k, EDGES:] = came_ref[k, HALF:]


def unpack_kernel(where_am_i, side, half_ref, *refs):
    qkv_ref, out_ref = refs[3:5] if side else refs[:2]
    wide_s, sems = refs[-2:]
    core = where_am_i()[1]
    low = core == side

    def store(start):
        for block in range(4):
            cols = slice(block * 256, (block + 1) * 256)
            if start:
                for k in range(4 * block, 4 * block + 4):
                    at = slice(k // 2 * 128, (k // 2 + 1) * 128)
                    wide_s[k % 2 * CHUNK : (k % 2 + 1) * CHUNK, at] = half_ref[moved_chunk(k), :CHUNK].astype(f32)

            def copy(ref, first):
                to = ref.at[:, first : first + 256]
                move = pltpu.make_async_copy(wide_s.at[:, cols], to, sems.at[block])
                move.start() if start else move.wait()

            pl.when(low)(lambda: copy(qkv_ref, block * 256))
            if block < 2:
                pl.when(jnp.logical_not(low))(lambda: copy(qkv_ref, 2 * D + block * 256))
            else:
                pl.when(jnp.logical_not(low))(lambda: copy(out_ref, block * 256 - D))

    if side:
        own_ref, gain_ref, gain_s, gain_sem = refs[0], refs[5], *refs[6:8]
        at = moved_chunk(0)
        gain = half_ref[at, CHUNK:].astype(f32) + own_ref[at, CHUNK:].astype(f32)
        for k in range(4):
            gain_s[:, k * 128 : (k + 1) * 128] = gain[k : k + 1, :]
        move = pltpu.make_async_copy(gain_s, gain_ref, gain_sem)
        move.start()
    store(True)
    store(False)
    if side:
        move.wait()


def unpack(where_am_i, side, half, *rest):
    whole = pl.BlockSpec(memory_space=pltpu.VMEM)
    stay = pl.BlockSpec(memory_space=pltpu.HBM)
    outs = [shape(D, 3 * D, dtype=f32), shape(D, D, dtype=f32)]
    return pl.pallas_call(
        functools.partial(unpack_kernel, where_am_i, side),
        out_shape=outs + [shape(1, D, dtype=f32)] * side,
        in_specs=[whole] + [whole, stay, stay] * side,
        out_specs=[stay] * (2 + side),
        scratch_shapes=[pltpu.VMEM((1, D), f32), pltpu.SemaphoreType.DMA] * side
        + [pltpu.VMEM((D, 2 * D), f32), pltpu.SemaphoreType.DMA((4,))],
        input_output_aliases={2: 0, 3: 1} if side else {},
        compiler_params=pltpu.CompilerParams(vmem_limit_bytes=12 * 1024 * 1024),
        cost_estimate=pl.CostEstimate(flops=1_000_000, bytes_accessed=3_000_000, transcendentals=0),
    )(half, *rest)


def place_kernel(own_ref, came_ref, edge_ref, mixed_ref, d_latent_ref):
    for k, out_ref in enumerate((mixed_ref, d_latent_ref)):
        for r in range(3):
            at = r * TILE[1]
            for first, body_ref, edges in ((0, came_ref, EDGES), (HALF, own_ref, 0)):
                edge = edge_ref[k, edges + r * EDGE : edges + (r + 1) * EDGE].astype(f32)
                body = body_ref[k, at : at + EDGE].astype(f32)
                out_ref[first + at : first + at + EDGE, :] = (body + edge).astype(bf16)
                out_ref[first + at + EDGE : first + at + TILE[1], :] = body_ref[k, at + EDGE : at + TILE[1]]


def shifted(lat_by, lon_by):
    pairs = []
    for i in range(256):
        lat, lon = i // 32, i % 32
        pairs.append((i, (lat + lat_by) % 8 * 32 + (lon + lon_by) % 32))
    return pairs


def swapped(bits):
    return [(i, i ^ bits) for i in range(256)]


def send(value, pairs):
    return lax.ppermute(value, ALL, pairs)


def sum_and_return(other, operands, finished):
    arrived = send(other, swapped(1))
    own, back, back_lon, chunks = add(here, arrived, operands, finished)
    pieces = lax.all_to_all(chunks, BOX, 0, 0, tiled=True)
    total = jnp.sum(pieces.astype(f32), axis=0).astype(bf16)
    for bits in (192, 4, 12):
        total = (total.astype(f32) + send(total, swapped(bits)).astype(f32)).astype(bf16)
    came = send(back, shifted(1, 0))
    edge = vmem_call(edge_kernel, [shape(2, 2 * EDGES, D)], [], 1_000_000, 1_000_000, 2)(came, back_lon)[0]
    total, edge = lax.optimization_barrier((total, edge))
    half = lax.all_to_all(jnp.broadcast_to(total, (16, SUMMED, 128)), BOX, 0, 0, tiled=True)
    edge = send(edge, shifted(0, 1))
    mixed, d_latent = vmem_call(
        place_kernel, [shape(2 * HALF, D), shape(2 * HALF, D)], [], 1_000_000, 2_000_000, 3
    )(own, came, edge)
    half, mixed, d_latent = lax.optimization_barrier((half, mixed, d_latent))
    arrived = send(half, swapped(1))
    parts = unpack(here, 0, half)
    grad_qkv, grad_out, grad_gain = unpack(here, 1, arrived, half, *parts)
    return mixed.reshape(*TILE, D), d_latent.reshape(*TILE, D), grad_qkv, grad_out, grad_gain.reshape(D)


def local(latent, norm_gain, w_qkv, w_out, cotangent):
    both = jnp.stack([latent[:3], cotangent[:3]])
    halo_lat = send(both.reshape(2, HALF, D), shifted(-1, 0))
    edge = jnp.stack([latent[3:, :16], cotangent[3:, :16]])
    to_cor, to_lon = vmem_call(
        edges_kernel, [shape(2, EDGES, D), shape(2, EDGES, D)], [], 1_000_000, 500_000, 2
    )(both, edge)
    halo_cor = send(to_cor, shifted(-1, -1))
    halo_lon = send(to_lon, shifted(0, -1))
    return sum_and_return(*block(
        here, latent.reshape(-1, D), cotangent.reshape(-1, D), halo_lat, halo_lon, halo_cor,
        norm_gain.reshape(1, D), w_qkv, w_out,
    ))


def solution(mesh):
    fine = Mesh(mesh.devices.reshape((2,) * 8), ALL)
    in_specs = (P(LAT, LON, None), P(), P(), P(), P(LAT, LON, None))
    out_specs = (P(LAT, LON, None), P(LAT, LON, None), P(), P(), P())
    return jax.shard_map(local, mesh=fine, in_specs=in_specs, out_specs=out_specs, check_vma=False)
```

```python
import functools

import jax
import jax.numpy as jnp
from jax import lax
from jax.experimental import pallas as pl
from jax.experimental.pallas import tpu as pltpu
from jax.sharding import Mesh, PartitionSpec as P

ALL = ("xh", "xl", "yh", "yl", "zh", "zm", "zl", "c")
LAT = ALL[:3]
LON = ALL[3:]
BOX = ("xh", "xl", "yl", "zl")
HEADS = 16
HS = 32
WL = 6
WW = 12
TILE = (6, 48)
D = 512
WINDOWS = 4
ROWS = 80
TOKENS = WINDOWS * ROWS
GROUP = 8
SPAN = GROUP * HS
EDGE = 8
HALF = 3 * TILE[1]
EDGES = 3 * EDGE
STRIP = 512 * 8
CHUNK = STRIP // 16
SUMMED = CHUNK + 8
BACK = HALF + EDGES
f32 = jnp.float32
bf16 = jnp.bfloat16
NT = (((1,), (1,)), ((), ()))
TN = (((0,), (0,)), ((), ()))


def dot(a, b, dims=(((1,), (0,)), ((), ()))):
    return lax.dot_general(a, b, dims, preferred_element_type=f32)


def norm(latent):
    centred = latent - jnp.mean(latent, axis=-1, keepdims=True)
    variance = jnp.mean(centred * centred, axis=-1, keepdims=True)
    recip_std = lax.rsqrt(variance + 1e-05)
    return centred * recip_std, recip_std


def edges_kernel(rows_ref, edge_ref, to_cor_ref, to_lon_ref):
    for k in range(2):
        for r in range(3):
            at = slice(r * EDGE, (r + 1) * EDGE)
            to_cor_ref[k, at] = rows_ref[k, r, :EDGE]
            to_lon_ref[k, at] = edge_ref[k, r, :EDGE]


def prepare_kernel(w_qkv_ref, w_out_ref, picks_ref, w_qkv_s, w_out_s):
    w_qkv_s[...] = w_qkv_ref[...]
    w_out_s[...] = w_out_ref[...]
    def count(value, step, upto):
        return sum(jnp.where(value >= step * k, 1, 0) for k in range(1, upto))

    row = lax.broadcasted_iota(jnp.int32, (TOKENS, 128), 0)
    window = count(row, ROWS, WINDOWS)
    cell = row - window * ROWS
    line = count(cell, WW, WL)
    col = (window + 0) * WW + cell - line * WW + WW // 2
    below = line >= WL // 2
    line = jnp.where(below, line - WL // 2, line)
    inside = line * TILE[1] + col + jnp.where(below, HALF, 0)
    beyond = 2 * HALF + line * EDGE + col - TILE[1] + jnp.where(below, EDGES, 0)
    at = jnp.where(col < TILE[1], inside, beyond)
    at = jnp.where(cell < WL * WW, at, -1)
    lane = lax.broadcasted_iota(jnp.int32, (TOKENS, 128), 1)
    for k in range(3):
        picks_ref[:, k * 128 : (k + 1) * 128] = jnp.where(at == lane + k * 128, 1.0, 0.0).astype(bf16)


def weight_grads(side, scaled_ref, ctx_ref, cot_ref, dpacked_ref, to_ref):
    for block in range(4):
        if side and block > 1:
            pair = ctx_ref[...], cot_ref[:, (block - 2) * 256 : (block - 1) * 256]
        else:
            first = side * 2 * D + block * 256
            pair = scaled_ref[...], dpacked_ref[:, first : first + 256]
        part = dot(*pair, TN).astype(bf16)
        for k in range(2):
            at = (2 * block + k) * D
            to_ref[at : at + D, :] = part[:, k * 128 : (k + 1) * 128]


def attend_kernel(
    where_am_i,
    lat_ref, cot_ref, halo_lat_ref, halo_lon_ref, halo_cor_ref, gain_ref, w_qkv_ref, w_out_ref, picks_ref,
    other_ref, latent_s, cot_s, ctx_s, dpacked_s, scaled_s,
    packed_s, dctx_s,
):
    last_lat, core = where_am_i()
    picks = picks_ref[...]

    def gather(own, at):
        stack = jnp.concatenate(
            [own[HALF:, :], halo_lat_ref[at], halo_lon_ref[at], halo_cor_ref[at], jnp.zeros((48, D), bf16)],
            axis=0,
        )
        return dot(picks, stack)

    latent = gather(lat_ref, 0)
    latent_s[...] = latent.astype(bf16)
    cot_s[...] = gather(cot_ref, 1).astype(bf16)
    normed, _ = norm(latent)
    scaled_s[...] = (normed * gain_ref[...]).astype(bf16)
    packed_s[...] = dot(scaled_s[...], w_qkv_ref[...]).astype(bf16)
    dctx_s[...] = dot(cot_s[...], w_out_ref[...], NT).astype(bf16)

    scaling = HS ** (-0.5)
    key_at = lax.broadcasted_iota(jnp.int32, (ROWS, GROUP * ROWS), 0)
    lane = lax.broadcasted_iota(jnp.int32, (1, GROUP * ROWS), 1)
    query_at = lane
    for h in range(1, GROUP):
        query_at = query_at - jnp.where(lane >= h * ROWS, ROWS, 0)
    split = WL // 2 * WW
    differ = jnp.logical_and(last_lat, (key_at >= split) != (query_at >= split))
    excluded = jnp.logical_or(key_at >= WL * WW, differ)
    bias = jnp.where(excluded, -1e30, 0.0).astype(f32)
    head_of = lax.broadcasted_iota(jnp.int32, (GROUP, 1, SPAN), 2) // HS
    head = lax.broadcasted_iota(jnp.int32, (GROUP, 1, SPAN), 0)
    own_head = jnp.where(head_of == head, 1.0, 0.0).astype(f32)
    own_head_b = own_head.astype(bf16)

    def spread(rows):
        return (rows[None] * own_head_b).reshape(GROUP * ROWS, SPAN)

    def collect(rows):
        return jnp.sum(rows.reshape(GROUP, ROWS, SPAN) * own_head, axis=0).astype(bf16)

    def begin(w, g):
        rows = slice(w * ROWS, (w + 1) * ROWS)
        at = [slice(b * D + g * SPAN, b * D + (g + 1) * SPAN) for b in range(3)]
        keys = packed_s[rows, at[1]]
        values = packed_s[rows, at[2]]
        queries = spread(packed_s[rows, at[0]])
        d_context = spread(dctx_s[rows, at[0]])
        return rows, at, keys, values, queries, d_context, dot(keys, queries, NT), dot(values, d_context, NT)

    def end(rows, at, keys, values, queries, d_context, scores, d_weights):
        scores = scores * (scaling * 1.4426950408889634) + bias
        expo = jnp.exp2(scores - jnp.max(scores, axis=0, keepdims=True))
        probs = expo * (1.0 / jnp.sum(expo, axis=0, keepdims=True))
        weights = probs.astype(bf16)
        mean_d = jnp.sum(d_weights * probs, axis=0, keepdims=True)
        d_scaled = ((probs * scaling) * (d_weights - mean_d)).astype(bf16)
        ctx_s[rows, at[0]] = collect(dot(weights, values, TN))
        dpacked_s[rows, at[2]] = dot(weights, d_context).astype(bf16)
        dpacked_s[rows, at[0]] = collect(dot(d_scaled, keys, TN))
        dpacked_s[rows, at[1]] = dot(d_scaled, queries).astype(bf16)

    todo = [(w, g) for w in range(WINDOWS) for g in range(HEADS // GROUP)]
    begun = begin(*todo[0])
    for k in range(1, len(todo) + 1):
        later = begin(*todo[k]) if k < len(todo) else None
        end(*begun)
        begun = later

    pl.when(core == 1)(lambda: weight_grads(0, scaled_s, ctx_s, cot_s, dpacked_s, other_ref))
    pl.when(core == 0)(lambda: weight_grads(1, scaled_s, ctx_s, cot_s, dpacked_s, other_ref))


def finish(
    side,
    latent_ref, cot_ref, ctx_ref, dpacked_ref, scaled_ref, gain_ref, w_qkv_ref, w_out_ref, picks_ref,
    own_ref, back_ref, back_lon_ref, gain_rows_ref, mine_ref,
):
    weight_grads(side, scaled_ref, ctx_ref, cot_ref, dpacked_ref, mine_ref)
    latent = latent_ref[...].astype(f32)
    normed, recip_std = norm(latent)
    d_shifted = dot(dpacked_ref[...], w_qkv_ref[...], NT).astype(bf16).astype(f32)
    grad_gain = jnp.sum(d_shifted * normed, axis=0, keepdims=True)
    gain_rows_ref[...] = jnp.concatenate(
        [grad_gain[:, k * 128 : (k + 1) * 128] for k in range(4)] + [jnp.zeros((4, 128), f32)], axis=0
    ).astype(bf16)
    hidden = d_shifted * gain_ref[...]
    part = recip_std * (
        hidden
        - jnp.mean(hidden, axis=-1, keepdims=True)
        - normed * jnp.mean(hidden * normed, axis=-1, keepdims=True)
    )
    d_latent = (cot_ref[...].astype(f32) + part).astype(bf16)
    attn = dot(ctx_ref[...], w_out_ref[...]).astype(bf16).astype(f32)
    mixed = (latent + attn).astype(bf16)
    picks = picks_ref[...]
    for k, value in enumerate((mixed, d_latent)):
        moved = dot(picks, value, TN).astype(bf16)
        own_ref[k] = moved[:HALF]
        back_ref[k, :HALF] = moved[HALF : 2 * HALF]
        back_ref[k, HALF:] = moved[2 * HALF + EDGES : 2 * HALF + 2 * EDGES]
        back_lon_ref[k] = moved[2 * HALF : 2 * HALF + EDGES]


def finish_kernel(where_am_i, *refs):
    pl.when(where_am_i()[1] == 1)(lambda: finish(1, *refs))


def here():
    last_lat = lax.axis_index("xh") + lax.axis_index("xl") + lax.axis_index("yh") == 3
    return last_lat, lax.axis_index("c")


def moved_chunk(k):
    return k + ((k ^ 2) - k) * lax.axis_index("yh")


def vmem_call(kernel, out_shapes, scratch, flops, moved, count, mebibytes=12):
    whole = pl.BlockSpec(memory_space=pltpu.VMEM)
    return pl.pallas_call(
        kernel,
        out_shape=out_shapes,
        in_specs=[whole] * count,
        out_specs=[whole] * len(out_shapes),
        scratch_shapes=scratch,
        compiler_params=pltpu.CompilerParams(vmem_limit_bytes=mebibytes * 1024 * 1024),
        cost_estimate=pl.CostEstimate(flops=flops, bytes_accessed=moved, transcendentals=0),
    )


def shape(*dims, dtype=bf16):
    return jax.ShapeDtypeStruct(dims, dtype)


FINISHED = [shape(2, HALF, D), shape(2, BACK, D), shape(2, EDGES, D), shape(8, 128), shape(STRIP, 128)]


def block(where_am_i, latent, cot, halo_lat, halo_lon, halo_cor, gain, w_qkv, w_out):
    picks, w_qkv, w_out = vmem_call(
        prepare_kernel, [shape(TOKENS, 384), shape(D, 3 * D), shape(D, D)], [], 1_000_000, 4_000_000, 2
    )(w_qkv, w_out)
    other, *kept = vmem_call(
        functools.partial(attend_kernel, where_am_i),
        [
            shape(STRIP, 128),
            shape(TOKENS, D), shape(TOKENS, D), shape(TOKENS, D), shape(TOKENS, 3 * D), shape(TOKENS, D),
        ],
        [pltpu.VMEM((TOKENS, 3 * D), bf16), pltpu.VMEM((TOKENS, D), bf16)],
        5_000_000_000, 8_000_000, 9, 32,
    )(latent, cot, halo_lat, halo_lon, halo_cor, gain, w_qkv, w_out, picks)
    operands = (*kept, gain, w_qkv, w_out, picks)
    finished = vmem_call(
        functools.partial(finish_kernel, where_am_i), FINISHED, [], 1_500_000_000, 4_000_000, 9, 24
    )(*operands)
    return other, operands, finished


def add_kernel(where_am_i, arrived_ref, *refs):
    operands, early, outs = refs[:9], refs[9:14], refs[14:17]
    chunks_ref, gain_s, mine_s = refs[17:]
    core = where_am_i()[1]

    def add_to_arrived(gain_ref, mine_ref):
        for k in range(16):
            at = slice(k * CHUNK, (k + 1) * CHUNK)
            to = moved_chunk(k)
            chunks_ref[to, :CHUNK] = (mine_ref[at, :].astype(f32) + arrived_ref[at, :].astype(f32)).astype(bf16)
            chunks_ref[to, CHUNK:] = gain_ref[...]

    @pl.when(core == 0)
    def _():
        finish(0, *operands, *outs, gain_s, mine_s)
        add_to_arrived(gain_s, mine_s)

    @pl.when(core == 1)
    def _():
        add_to_arrived(*early[3:])
        for out_ref, early_ref in zip(outs, early):
            out_ref[...] = early_ref[...]


def add(where_am_i, arrived, operands, finished):
    whole = pl.BlockSpec(memory_space=pltpu.VMEM)
    return pl.pallas_call(
        functools.partial(add_kernel, where_am_i),
        out_shape=FINISHED[:3] + [shape(16, SUMMED, 128)],
        in_specs=[whole] * 15,
        out_specs=[whole] * 4,
        scratch_shapes=[pltpu.VMEM((8, 128), bf16), pltpu.VMEM((STRIP, 128), bf16)],
        compiler_params=pltpu.CompilerParams(vmem_limit_bytes=24 * 1024 * 1024),
        cost_estimate=pl.CostEstimate(flops=1_500_000_000, bytes_accessed=4_000_000, transcendentals=0),
    )(arrived, *operands, *finished)


def edge_kernel(came_ref, back_lon_ref, edge_ref):
    for k in range(2):
        edge_ref[k, :EDGES] = back_lon_ref[k]
        edge_ref[k, EDGES:] = came_ref[k, HALF:]


def unpack_kernel(where_am_i, side, half_ref, *refs):
    qkv_ref, out_ref = refs[3:5] if side else refs[:2]
    wide_s, sems = refs[-2:]
    core = where_am_i()[1]
    low = core == side

    def store(start):
        for block in range(4):
            cols = slice(block * 256, (block + 1) * 256)
            if start:
                for k in range(4 * block, 4 * block + 4):
                    at = slice(k // 2 * 128, (k // 2 + 1) * 128)
                    wide_s[k % 2 * CHUNK : (k % 2 + 1) * CHUNK, at] = half_ref[moved_chunk(k), :CHUNK].astype(f32)

            def copy(ref, first):
                to = ref.at[:, first : first + 256]
                move = pltpu.make_async_copy(wide_s.at[:, cols], to, sems.at[block])
                move.start() if start else move.wait()

            pl.when(low)(lambda: copy(qkv_ref, block * 256))
            if block < 2:
                pl.when(jnp.logical_not(low))(lambda: copy(qkv_ref, 2 * D + block * 256))
            else:
                pl.when(jnp.logical_not(low))(lambda: copy(out_ref, block * 256 - D))

    if side:
        own_ref, gain_ref, gain_s, gain_sem = refs[0], refs[5], *refs[6:8]
        at = moved_chunk(0)
        gain = half_ref[at, CHUNK:].astype(f32) + own_ref[at, CHUNK:].astype(f32)
        for k in range(4):
            gain_s[:, k * 128 : (k + 1) * 128] = gain[k : k + 1, :]
        move = pltpu.make_async_copy(gain_s, gain_ref, gain_sem)
        move.start()
    store(True)
    store(False)
    if side:
        move.wait()


def unpack(where_am_i, side, half, *rest):
    whole = pl.BlockSpec(memory_space=pltpu.VMEM)
    stay = pl.BlockSpec(memory_space=pltpu.HBM)
    outs = [shape(D, 3 * D, dtype=f32), shape(D, D, dtype=f32)]
    return pl.pallas_call(
        functools.partial(unpack_kernel, where_am_i, side),
        out_shape=outs + [shape(1, D, dtype=f32)] * side,
        in_specs=[whole] + [whole, stay, stay] * side,
        out_specs=[stay] * (2 + side),
        scratch_shapes=[pltpu.VMEM((1, D), f32), pltpu.SemaphoreType.DMA] * side
        + [pltpu.VMEM((D, 2 * D), f32), pltpu.SemaphoreType.DMA((4,))],
        input_output_aliases={2: 0, 3: 1} if side else {},
        compiler_params=pltpu.CompilerParams(vmem_limit_bytes=12 * 1024 * 1024),
        cost_estimate=pl.CostEstimate(flops=1_000_000, bytes_accessed=3_000_000, transcendentals=0),
    )(half, *rest)


def place_kernel(own_ref, came_ref, edge_ref, mixed_ref, d_latent_ref):
    for k, out_ref in enumerate((mixed_ref, d_latent_ref)):
        for r in range(3):
            at = r * TILE[1]
            for first, body_ref, edges in ((0, came_ref, EDGES), (HALF, own_ref, 0)):
                edge = edge_ref[k, edges + r * EDGE : edges + (r + 1) * EDGE].astype(f32)
                body = body_ref[k, at : at + EDGE].astype(f32)
                out_ref[first + at : first + at + EDGE, :] = (body + edge).astype(bf16)
                out_ref[first + at + EDGE : first + at + TILE[1], :] = body_ref[k, at + EDGE : at + TILE[1]]


def shifted(lat_by, lon_by):
    pairs = []
    for i in range(256):
        lat, lon = i // 32, i % 32
        pairs.append((i, (lat + lat_by) % 8 * 32 + (lon + lon_by) % 32))
    return pairs


def swapped(bits):
    return [(i, i ^ bits) for i in range(256)]


def send(value, pairs):
    return lax.ppermute(value, ALL, pairs)


def sum_and_return(other, operands, finished):
    arrived = send(other, swapped(1))
    own, back, back_lon, chunks = add(here, arrived, operands, finished)
    pieces = lax.all_to_all(chunks, BOX, 0, 0, tiled=True)
    total = jnp.sum(pieces.astype(f32), axis=0).astype(bf16)
    for bits in (48, 4, 12):
        total = (total.astype(f32) + send(total, swapped(bits)).astype(f32)).astype(bf16)
    came = send(back, shifted(1, 0))
    edge = vmem_call(edge_kernel, [shape(2, 2 * EDGES, D)], [], 1_000_000, 1_000_000, 2)(came, back_lon)[0]
    total, edge = lax.optimization_barrier((total, edge))
    half = lax.all_to_all(jnp.broadcast_to(total, (16, SUMMED, 128)), BOX, 0, 0, tiled=True)
    edge = send(edge, shifted(0, 1))
    mixed, d_latent = vmem_call(
        place_kernel, [shape(2 * HALF, D), shape(2 * HALF, D)], [], 1_000_000, 2_000_000, 3
    )(own, came, edge)
    half, mixed, d_latent = lax.optimization_barrier((half, mixed, d_latent))
    arrived = send(half, swapped(1))
    parts = unpack(here, 0, half)
    grad_qkv, grad_out, grad_gain = unpack(here, 1, arrived, half, *parts)
    return mixed.reshape(*TILE, D), d_latent.reshape(*TILE, D), grad_qkv, grad_out, grad_gain.reshape(D)


def local(latent, norm_gain, w_qkv, w_out, cotangent):
    both = jnp.stack([latent[:3], cotangent[:3]])
    halo_lat = send(both.reshape(2, HALF, D), shifted(-1, 0))
    edge = jnp.stack([latent[3:, :16], cotangent[3:, :16]])
    to_cor, to_lon = vmem_call(
        edges_kernel, [shape(2, EDGES, D), shape(2, EDGES, D)], [], 1_000_000, 500_000, 2
    )(both, edge)
    halo_cor = send(to_cor, shifted(-1, -1))
    halo_lon = send(to_lon, shifted(0, -1))
    return sum_and_return(*block(
        here, latent.reshape(-1, D), cotangent.reshape(-1, D), halo_lat, halo_lon, halo_cor,
        norm_gain.reshape(1, D), w_qkv, w_out,
    ))


def solution(mesh):
    fine = Mesh(mesh.devices.reshape((2,) * 8), ALL)
    in_specs = (P(LAT, LON, None), P(), P(), P(), P(LAT, LON, None))
    out_specs = (P(LAT, LON, None), P(LAT, LON, None), P(), P(), P())
    return jax.shard_map(local, mesh=fine, in_specs=in_specs, out_specs=out_specs, check_vma=False)
```

```python
import functools

import jax
import jax.numpy as jnp
from jax import lax
from jax.experimental import pallas as pl
from jax.experimental.pallas import tpu as pltpu
from jax.sharding import Mesh, PartitionSpec as P

ALL = ("xh", "xl", "yh", "yl", "zh", "zm", "zl", "c")
LAT = ALL[:3]
LON = ALL[3:]
BOX = ("xl", "yh", "yl", "zl")
HEADS = 16
HS = 32
WL = 6
WW = 12
TILE = (6, 48)
D = 512
WINDOWS = 4
ROWS = 80
TOKENS = WINDOWS * ROWS
GROUP = 8
SPAN = GROUP * HS
EDGE = 8
HALF = 3 * TILE[1]
EDGES = 3 * EDGE
STRIP = 512 * 8
CHUNK = STRIP // 16
SUMMED = CHUNK + 8
BACK = HALF + EDGES
f32 = jnp.float32
bf16 = jnp.bfloat16
NT = (((1,), (1,)), ((), ()))
TN = (((0,), (0,)), ((), ()))


def dot(a, b, dims=(((1,), (0,)), ((), ()))):
    return lax.dot_general(a, b, dims, preferred_element_type=f32)


def norm(latent):
    centred = latent - jnp.mean(latent, axis=-1, keepdims=True)
    variance = jnp.mean(centred * centred, axis=-1, keepdims=True)
    recip_std = lax.rsqrt(variance + 1e-05)
    return centred * recip_std, recip_std


def edges_kernel(rows_ref, edge_ref, to_cor_ref, to_lon_ref):
    for k in range(2):
        for r in range(3):
            at = slice(r * EDGE, (r + 1) * EDGE)
            to_cor_ref[k, at] = rows_ref[k, r, :EDGE]
            to_lon_ref[k, at] = edge_ref[k, r, :EDGE]


def prepare_kernel(w_qkv_ref, w_out_ref, picks_ref, w_qkv_s, w_out_s):
    w_qkv_s[...] = w_qkv_ref[...]
    w_out_s[...] = w_out_ref[...]
    def count(value, step, upto):
        return sum(jnp.where(value >= step * k, 1, 0) for k in range(1, upto))

    row = lax.broadcasted_iota(jnp.int32, (TOKENS, 128), 0)
    window = count(row, ROWS, WINDOWS)
    cell = row - window * ROWS
    line = count(cell, WW, WL)
    col = (window + 0) * WW + cell - line * WW + WW // 2
    below = line >= WL // 2
    line = jnp.where(below, line - WL // 2, line)
    inside = line * TILE[1] + col + jnp.where(below, HALF, 0)
    beyond = 2 * HALF + line * EDGE + col - TILE[1] + jnp.where(below, EDGES, 0)
    at = jnp.where(col < TILE[1], inside, beyond)
    at = jnp.where(cell < WL * WW, at, -1)
    lane = lax.broadcasted_iota(jnp.int32, (TOKENS, 128), 1)
    for k in range(3):
        picks_ref[:, k * 128 : (k + 1) * 128] = jnp.where(at == lane + k * 128, 1.0, 0.0).astype(bf16)


def weight_grads(side, scaled_ref, ctx_ref, cot_ref, dpacked_ref, to_ref):
    for block in range(4):
        if side and block > 1:
            pair = ctx_ref[...], cot_ref[:, (block - 2) * 256 : (block - 1) * 256]
        else:
            first = side * 2 * D + block * 256
            pair = scaled_ref[...], dpacked_ref[:, first : first + 256]
        part = dot(*pair, TN).astype(bf16)
        for k in range(2):
            at = (2 * block + k) * D
            to_ref[at : at + D, :] = part[:, k * 128 : (k + 1) * 128]


def attend_kernel(
    where_am_i,
    lat_ref, cot_ref, halo_lat_ref, halo_lon_ref, halo_cor_ref, gain_ref, w_qkv_ref, w_out_ref, picks_ref,
    other_ref, latent_s, cot_s, ctx_s, dpacked_s, scaled_s,
    packed_s, dctx_s,
):
    last_lat, core = where_am_i()
    picks = picks_ref[...]

    def gather(own, at):
        stack = jnp.concatenate(
            [own[HALF:, :], halo_lat_ref[at], halo_lon_ref[at], halo_cor_ref[at], jnp.zeros((48, D), bf16)],
            axis=0,
        )
        return dot(picks, stack)

    latent = gather(lat_ref, 0)
    latent_s[...] = latent.astype(bf16)
    cot_s[...] = gather(cot_ref, 1).astype(bf16)
    normed, _ = norm(latent)
    scaled_s[...] = (normed * gain_ref[...]).astype(bf16)
    packed_s[...] = dot(scaled_s[...], w_qkv_ref[...]).astype(bf16)
    dctx_s[...] = dot(cot_s[...], w_out_ref[...], NT).astype(bf16)

    scaling = HS ** (-0.5)
    key_at = lax.broadcasted_iota(jnp.int32, (ROWS, GROUP * ROWS), 0)
    lane = lax.broadcasted_iota(jnp.int32, (1, GROUP * ROWS), 1)
    query_at = lane
    for h in range(1, GROUP):
        query_at = query_at - jnp.where(lane >= h * ROWS, ROWS, 0)
    split = WL // 2 * WW
    differ = jnp.logical_and(last_lat, (key_at >= split) != (query_at >= split))
    excluded = jnp.logical_or(key_at >= WL * WW, differ)
    bias = jnp.where(excluded, -1e30, 0.0).astype(f32)
    head_of = lax.broadcasted_iota(jnp.int32, (GROUP, 1, SPAN), 2) // HS
    head = lax.broadcasted_iota(jnp.int32, (GROUP, 1, SPAN), 0)
    own_head = jnp.where(head_of == head, 1.0, 0.0).astype(f32)
    own_head_b = own_head.astype(bf16)

    def spread(rows):
        return (rows[None] * own_head_b).reshape(GROUP * ROWS, SPAN)

    def collect(rows):
        return jnp.sum(rows.reshape(GROUP, ROWS, SPAN) * own_head, axis=0).astype(bf16)

    def begin(w, g):
        rows = slice(w * ROWS, (w + 1) * ROWS)
        at = [slice(b * D + g * SPAN, b * D + (g + 1) * SPAN) for b in range(3)]
        keys = packed_s[rows, at[1]]
        values = packed_s[rows, at[2]]
        queries = spread(packed_s[rows, at[0]])
        d_context = spread(dctx_s[rows, at[0]])
        return rows, at, keys, values, queries, d_context, dot(keys, queries, NT), dot(values, d_context, NT)

    def end(rows, at, keys, values, queries, d_context, scores, d_weights):
        scores = scores * (scaling * 1.4426950408889634) + bias
        expo = jnp.exp2(scores - jnp.max(scores, axis=0, keepdims=True))
        probs = expo * (1.0 / jnp.sum(expo, axis=0, keepdims=True))
        weights = probs.astype(bf16)
        mean_d = jnp.sum(d_weights * probs, axis=0, keepdims=True)
        d_scaled = ((probs * scaling) * (d_weights - mean_d)).astype(bf16)
        ctx_s[rows, at[0]] = collect(dot(weights, values, TN))
        dpacked_s[rows, at[2]] = dot(weights, d_context).astype(bf16)
        dpacked_s[rows, at[0]] = collect(dot(d_scaled, keys, TN))
        dpacked_s[rows, at[1]] = dot(d_scaled, queries).astype(bf16)

    todo = [(w, g) for w in range(WINDOWS) for g in range(HEADS // GROUP)]
    begun = begin(*todo[0])
    for k in range(1, len(todo) + 1):
        later = begin(*todo[k]) if k < len(todo) else None
        end(*begun)
        begun = later

    pl.when(core == 1)(lambda: weight_grads(0, scaled_s, ctx_s, cot_s, dpacked_s, other_ref))
    pl.when(core == 0)(lambda: weight_grads(1, scaled_s, ctx_s, cot_s, dpacked_s, other_ref))


def finish(
    side,
    latent_ref, cot_ref, ctx_ref, dpacked_ref, scaled_ref, gain_ref, w_qkv_ref, w_out_ref, picks_ref,
    own_ref, back_ref, back_lon_ref, gain_rows_ref, mine_ref,
):
    weight_grads(side, scaled_ref, ctx_ref, cot_ref, dpacked_ref, mine_ref)
    latent = latent_ref[...].astype(f32)
    normed, recip_std = norm(latent)
    d_shifted = dot(dpacked_ref[...], w_qkv_ref[...], NT).astype(bf16).astype(f32)
    grad_gain = jnp.sum(d_shifted * normed, axis=0, keepdims=True)
    gain_rows_ref[...] = jnp.concatenate(
        [grad_gain[:, k * 128 : (k + 1) * 128] for k in range(4)] + [jnp.zeros((4, 128), f32)], axis=0
    ).astype(bf16)
    hidden = d_shifted * gain_ref[...]
    part = recip_std * (
        hidden
        - jnp.mean(hidden, axis=-1, keepdims=True)
        - normed * jnp.mean(hidden * normed, axis=-1, keepdims=True)
    )
    d_latent = (cot_ref[...].astype(f32) + part).astype(bf16)
    attn = dot(ctx_ref[...], w_out_ref[...]).astype(bf16).astype(f32)
    mixed = (latent + attn).astype(bf16)
    picks = picks_ref[...]
    for k, value in enumerate((mixed, d_latent)):
        moved = dot(picks, value, TN).astype(bf16)
        own_ref[k] = moved[:HALF]
        back_ref[k, :HALF] = moved[HALF : 2 * HALF]
        back_ref[k, HALF:] = moved[2 * HALF + EDGES : 2 * HALF + 2 * EDGES]
        back_lon_ref[k] = moved[2 * HALF : 2 * HALF + EDGES]


def finish_kernel(where_am_i, *refs):
    pl.when(where_am_i()[1] == 1)(lambda: finish(1, *refs))


def here():
    last_lat = lax.axis_index("xh") + lax.axis_index("xl") + lax.axis_index("yh") == 3
    return last_lat, lax.axis_index("c")


def moved_chunk(k):
    return lax.rem(k + 8 * lax.axis_index("xh"), 16)


def vmem_call(kernel, out_shapes, scratch, flops, moved, count, mebibytes=12):
    whole = pl.BlockSpec(memory_space=pltpu.VMEM)
    return pl.pallas_call(
        kernel,
        out_shape=out_shapes,
        in_specs=[whole] * count,
        out_specs=[whole] * len(out_shapes),
        scratch_shapes=scratch,
        compiler_params=pltpu.CompilerParams(vmem_limit_bytes=mebibytes * 1024 * 1024),
        cost_estimate=pl.CostEstimate(flops=flops, bytes_accessed=moved, transcendentals=0),
    )


def shape(*dims, dtype=bf16):
    return jax.ShapeDtypeStruct(dims, dtype)


FINISHED = [shape(2, HALF, D), shape(2, BACK, D), shape(2, EDGES, D), shape(8, 128), shape(STRIP, 128)]


def block(where_am_i, latent, cot, halo_lat, halo_lon, halo_cor, gain, w_qkv, w_out):
    picks, w_qkv, w_out = vmem_call(
        prepare_kernel, [shape(TOKENS, 384), shape(D, 3 * D), shape(D, D)], [], 1_000_000, 4_000_000, 2
    )(w_qkv, w_out)
    other, *kept = vmem_call(
        functools.partial(attend_kernel, where_am_i),
        [
            shape(STRIP, 128),
            shape(TOKENS, D), shape(TOKENS, D), shape(TOKENS, D), shape(TOKENS, 3 * D), shape(TOKENS, D),
        ],
        [pltpu.VMEM((TOKENS, 3 * D), bf16), pltpu.VMEM((TOKENS, D), bf16)],
        5_000_000_000, 8_000_000, 9, 32,
    )(latent, cot, halo_lat, halo_lon, halo_cor, gain, w_qkv, w_out, picks)
    operands = (*kept, gain, w_qkv, w_out, picks)
    finished = vmem_call(
        functools.partial(finish_kernel, where_am_i), FINISHED, [], 1_500_000_000, 4_000_000, 9, 24
    )(*operands)
    return other, operands, finished


def add_kernel(where_am_i, arrived_ref, *refs):
    operands, early, outs = refs[:9], refs[9:14], refs[14:17]
    chunks_ref, gain_s, mine_s = refs[17:]
    core = where_am_i()[1]

    def add_to_arrived(gain_ref, mine_ref):
        for k in range(16):
            at = slice(k * CHUNK, (k + 1) * CHUNK)
            to = moved_chunk(k)
            chunks_ref[to, :CHUNK] = (mine_ref[at, :].astype(f32) + arrived_ref[at, :].astype(f32)).astype(bf16)
            chunks_ref[to, CHUNK:] = gain_ref[...]

    @pl.when(core == 0)
    def _():
        finish(0, *operands, *outs, gain_s, mine_s)
        add_to_arrived(gain_s, mine_s)

    @pl.when(core == 1)
    def _():
        add_to_arrived(*early[3:])
        for out_ref, early_ref in zip(outs, early):
            out_ref[...] = early_ref[...]


def add(where_am_i, arrived, operands, finished):
    whole = pl.BlockSpec(memory_space=pltpu.VMEM)
    return pl.pallas_call(
        functools.partial(add_kernel, where_am_i),
        out_shape=FINISHED[:3] + [shape(16, SUMMED, 128)],
        in_specs=[whole] * 15,
        out_specs=[whole] * 4,
        scratch_shapes=[pltpu.VMEM((8, 128), bf16), pltpu.VMEM((STRIP, 128), bf16)],
        compiler_params=pltpu.CompilerParams(vmem_limit_bytes=24 * 1024 * 1024),
        cost_estimate=pl.CostEstimate(flops=1_500_000_000, bytes_accessed=4_000_000, transcendentals=0),
    )(arrived, *operands, *finished)


def edge_kernel(came_ref, back_lon_ref, edge_ref):
    for k in range(2):
        edge_ref[k, :EDGES] = back_lon_ref[k]
        edge_ref[k, EDGES:] = came_ref[k, HALF:]


def unpack_kernel(where_am_i, side, half_ref, *refs):
    qkv_ref, out_ref = refs[3:5] if side else refs[:2]
    wide_s, sems = refs[-2:]
    core = where_am_i()[1]
    low = core == side

    def store(start):
        for block in range(8):
            cols = slice(block * 128, (block + 1) * 128)
            if start:
                for k in range(2 * block, 2 * block + 2):
                    at = slice(k // 2 * 128, (k // 2 + 1) * 128)
                    wide_s[k % 2 * CHUNK : (k % 2 + 1) * CHUNK, at] = half_ref[moved_chunk(k), :CHUNK].astype(f32)

            def copy(ref, first):
                to = ref.at[:, first : first + 128]
                move = pltpu.make_async_copy(wide_s.at[:, cols], to, sems.at[block])
                move.start() if start else move.wait()

            pl.when(low)(lambda: copy(qkv_ref, block * 128))
            if block < 4:
                pl.when(jnp.logical_not(low))(lambda: copy(qkv_ref, 2 * D + block * 128))
            else:
                pl.when(jnp.logical_not(low))(lambda: copy(out_ref, block * 128 - D))

    if side:
        own_ref, gain_ref, gain_s, gain_sem = refs[0], refs[5], *refs[6:8]
        at = moved_chunk(0)
        gain = half_ref[at, CHUNK:].astype(f32) + own_ref[at, CHUNK:].astype(f32)
        for k in range(4):
            gain_s[:, k * 128 : (k + 1) * 128] = gain[k : k + 1, :]
        move = pltpu.make_async_copy(gain_s, gain_ref, gain_sem)
        move.start()
    store(True)
    store(False)
    if side:
        move.wait()


def unpack(where_am_i, side, half, *rest):
    whole = pl.BlockSpec(memory_space=pltpu.VMEM)
    stay = pl.BlockSpec(memory_space=pltpu.HBM)
    outs = [shape(D, 3 * D, dtype=f32), shape(D, D, dtype=f32)]
    return pl.pallas_call(
        functools.partial(unpack_kernel, where_am_i, side),
        out_shape=outs + [shape(1, D, dtype=f32)] * side,
        in_specs=[whole] + [whole, stay, stay] * side,
        out_specs=[stay] * (2 + side),
        scratch_shapes=[pltpu.VMEM((1, D), f32), pltpu.SemaphoreType.DMA] * side
        + [pltpu.VMEM((D, 2 * D), f32), pltpu.SemaphoreType.DMA((8,))],
        input_output_aliases={2: 0, 3: 1} if side else {},
        compiler_params=pltpu.CompilerParams(vmem_limit_bytes=12 * 1024 * 1024),
        cost_estimate=pl.CostEstimate(flops=1_000_000, bytes_accessed=3_000_000, transcendentals=0),
    )(half, *rest)


def place_kernel(own_ref, came_ref, edge_ref, mixed_ref, d_latent_ref):
    for k, out_ref in enumerate((mixed_ref, d_latent_ref)):
        for r in range(3):
            at = r * TILE[1]
            for first, body_ref, edges in ((0, came_ref, EDGES), (HALF, own_ref, 0)):
                edge = edge_ref[k, edges + r * EDGE : edges + (r + 1) * EDGE].astype(f32)
                body = body_ref[k, at : at + EDGE].astype(f32)
                out_ref[first + at : first + at + EDGE, :] = (body + edge).astype(bf16)
                out_ref[first + at + EDGE : first + at + TILE[1], :] = body_ref[k, at + EDGE : at + TILE[1]]


def shifted(lat_by, lon_by):
    pairs = []
    for i in range(256):
        lat, lon = i // 32, i % 32
        pairs.append((i, (lat + lat_by) % 8 * 32 + (lon + lon_by) % 32))
    return pairs


def swapped(bits):
    return [(i, i ^ bits) for i in range(256)]


def send(value, pairs):
    return lax.ppermute(value, ALL, pairs)


def sum_and_return(other, operands, finished):
    arrived = send(other, swapped(1))
    own, back, back_lon, chunks = add(here, arrived, operands, finished)
    pieces = lax.all_to_all(chunks, BOX, 0, 0, tiled=True)
    total = jnp.sum(pieces.astype(f32), axis=0).astype(bf16)
    for bits in (192, 4, 12):
        total = (total.astype(f32) + send(total, swapped(bits)).astype(f32)).astype(bf16)
    came = send(back, shifted(1, 0))
    edge = vmem_call(edge_kernel, [shape(2, 2 * EDGES, D)], [], 1_000_000, 1_000_000, 2)(came, back_lon)[0]
    total, edge = lax.optimization_barrier((total, edge))
    half = lax.all_to_all(jnp.broadcast_to(total, (16, SUMMED, 128)), BOX, 0, 0, tiled=True)
    edge = send(edge, shifted(0, 1))
    mixed, d_latent = vmem_call(
        place_kernel, [shape(2 * HALF, D), shape(2 * HALF, D)], [], 1_000_000, 2_000_000, 3
    )(own, came, edge)
    half, mixed, d_latent = lax.optimization_barrier((half, mixed, d_latent))
    arrived = send(half, swapped(1))
    parts = unpack(here, 0, half)
    grad_qkv, grad_out, grad_gain = unpack(here, 1, arrived, half, *parts)
    return mixed.reshape(*TILE, D), d_latent.reshape(*TILE, D), grad_qkv, grad_out, grad_gain.reshape(D)


def local(latent, norm_gain, w_qkv, w_out, cotangent):
    both = jnp.stack([latent[:3], cotangent[:3]])
    halo_lat = send(both.reshape(2, HALF, D), shifted(-1, 0))
    edge = jnp.stack([latent[3:, :16], cotangent[3:, :16]])
    to_cor, to_lon = vmem_call(
        edges_kernel, [shape(2, EDGES, D), shape(2, EDGES, D)], [], 1_000_000, 500_000, 2
    )(both, edge)
    halo_cor = send(to_cor, shifted(-1, -1))
    halo_lon = send(to_lon, shifted(0, -1))
    return sum_and_return(*block(
        here, latent.reshape(-1, D), cotangent.reshape(-1, D), halo_lat, halo_lon, halo_cor,
        norm_gain.reshape(1, D), w_qkv, w_out,
    ))


def solution(mesh):
    fine = Mesh(mesh.devices.reshape((2,) * 8), ALL)
    in_specs = (P(LAT, LON, None), P(), P(), P(), P(LAT, LON, None))
    out_specs = (P(LAT, LON, None), P(LAT, LON, None), P(), P(), P())
    return jax.shard_map(local, mesh=fine, in_specs=in_specs, out_specs=out_specs, check_vma=False)
```
